256 devices in a mesh: dp: 16 (over x_lo, z), seq: 16 (over y, x_hi, core).
Axes of the slice: x: 4 (x_hi: 2, x_lo: 2; x = x_hi * 2 + x_lo), y: 4, z: 8, core: 2. Of those that a mesh axis runs over, the one named last changes fastest.
Arguments:
- encoder_in: bfloat16 [131072, 768], P(('dp', 'seq')), parts along dimension 0, may hold values from -6 to 6
- conv_weight: bfloat16 [5, 768, 1536], P(None, 'seq'), may hold values from -0.09375 to 0.09375
- norm_gain: float32 [1536], replicated, may hold values from 0.1 to 1.9
- query_weight: bfloat16 [1536, 768], P('seq'), may hold values from -0.16 to 0.16
- key_weight: bfloat16 [1536, 768], P('seq'), may hold values from -3.4 to 3.4
- value_weight: bfloat16 [1536, 768], P('seq'), may hold values from -0.15625 to 0.15625
- out_weight: bfloat16 [768, 1536], P('seq'), may hold values from -0.21875 to 0.21875
- post_gain: float32 [1536], replicated, may hold values from 0.1 to 1.9
- left_weight: bfloat16 [1536, 128], replicated, may hold values from -0.625 to 0.625
- right_weight: bfloat16 [1536, 128], replicated, may hold values from -0.625 to 0.625
- pair_weight: bfloat16 [128, 128], replicated, may hold values from -1 to 1
- tile_ids: int32 [8448], P(('dp', 'seq')), parts along dimension 0, may hold values from 0 to 527, each once
Outputs:
- attended: bfloat16 [65536, 1536], P(('dp', 'seq')), parts along dimension 0
- pair_tiles: bfloat16 [8448, 8, 8, 128], P(('dp', 'seq')), parts along dimension 0
The draws below stay inside these ranges and needn't reach their ends.
There are 16 independent parts, one for each index of `dp`. The reference program is written for one: setup_inputs(seed, part) draws one part's arguments, and reference() takes and returns one part's arrays. A program takes and returns all parts, laid end to end along the dimension named above; an argument that names none is the same for every part. Nothing has to cross between parts.
Inputs may be any that keep to these rules, and one draw needn't show every extreme that they name: `tile_ids`: every tile number appears in exactly one slot of the part.
All inputs are finite; a program needn't handle non-finite values.
Results may differ from the reference program's by a relative error of at most 0.017.
Values may be sent and summed in bfloat16 or wider, within the bound.
No kernel may reach another device: no remote copies, remote signals or barrier semaphores. Data moves between devices by JAX's collectives and lax.ppermute only.
A program may use at most 384 MiB of HBM per device.

```python
import jax
import jax.numpy as jnp
import numpy as np
from jax import lax

CIN = 768
D = 1536
HEADS = 4
HD = 192
CP = 128
KW = 5
TOKENS = 4096
TILES = 528
N_SEQ = 16


def bounded_rows(key, salt):
    raw_rows = jax.random.truncated_normal(jax.random.fold_in(key, salt), -6.0, 6.0, (D, HEADS * HD), jnp.float32) * D ** (-0.5)
    return 0.16 * jnp.tanh(raw_rows / 0.16)


def draw_query_weight(key, part):
    return bounded_rows(key, 101).astype(jnp.bfloat16)


def draw_key_weight(key, part):
    key = jax.random.fold_in(key, 7)
    own_rows = 8.0 * bounded_rows(key, 1)
    return own_rows.astype(jnp.bfloat16)


def block_scale(stream_key, shape, shards, low, high):
    def one(axis_at, parts):
        heights = jax.random.uniform(jax.random.fold_in(jax.random.fold_in(stream_key, 6), axis_at), (parts,), jnp.float32, low / len(shards), high / len(shards))
        return jnp.repeat(jnp.exp(heights), shape[axis_at] // parts).reshape((-1,) + (1,) * (len(shape) - axis_at - 1))

    level = one(*shards[0])
    for cut in shards[1:]:
        level = level * one(*cut)
    return level


def centred(stream_key, dims, spread, most, pieces=(), kind=jnp.bfloat16):
    drawn = spread * jax.random.normal(stream_key, dims, jnp.float32)
    if pieces:
        drawn = drawn * block_scale(stream_key, dims, pieces, -0.22, 0.18)
    return jnp.clip(drawn, -most, most).astype(kind)


def setup_inputs(seed: int = 0, part: int = 0) -> dict:
    key_list = jax.random.split(jax.random.key(seed), 13)
    own_keys = jax.random.split(jax.random.fold_in(key_list[12], part), 13)
    encoder_in = centred(own_keys[0], (2 * TOKENS, CIN), 1.0, 6.0, ((0, 16),))
    conv_weight = centred(key_list[1], (KW, CIN, D), (KW * CIN) ** -0.5, 0.09375, ((1, 16),))
    norm_gain = jnp.clip(1.0 + 0.18 * jax.random.normal(key_list[2], (D,), jnp.float32), 0.1, 1.9)
    query_weight = draw_query_weight(jax.random.fold_in(key_list[12], 71), part)
    key_weight = draw_key_weight(jax.random.fold_in(key_list[12], 71), part)
    value_weight = centred(key_list[5], (D, HEADS * HD), D ** -0.5, 0.15625, ((0, 16),))
    out_weight = centred(key_list[6], (HEADS * HD, D), (HEADS * HD) ** -0.5, 0.21875, ((0, 16),))
    post_gain = jnp.clip(1.0 + 0.18 * jax.random.normal(key_list[7], (D,), jnp.float32), 0.1, 1.9)
    left_weight = centred(key_list[8], (D, CP), (D // 16) ** -0.5, 0.625)
    right_weight = centred(key_list[9], (D, CP), (D // 16) ** -0.5, 0.625)
    pair_weight = centred(key_list[10], (CP, CP), (CP // 4) ** -0.5, 1.0)
    tile_ids = jax.random.permutation(own_keys[11], TILES).astype(jnp.int32)
    return dict(encoder_in=encoder_in, conv_weight=conv_weight, norm_gain=norm_gain, query_weight=query_weight, key_weight=key_weight, value_weight=value_weight, out_weight=out_weight, post_gain=post_gain, left_weight=left_weight, right_weight=right_weight, pair_weight=pair_weight, tile_ids=tile_ids)


def root_norm(values_in, gain):
    return values_in * lax.rsqrt(lax.optimization_barrier(jnp.mean(values_in * values_in, axis=-1, keepdims=True)) + 1e-06) * gain.astype(jnp.float32)

def reference(encoder_in, conv_weight, norm_gain, query_weight, key_weight, value_weight, out_weight, post_gain, left_weight, right_weight, pair_weight, tile_ids):
    in_rows = encoder_in.shape[0]
    width = conv_weight.shape[2]
    padded = jnp.pad(encoder_in, ((2, 2), (0, 0)))
    conv_sum = jnp.zeros((in_rows, width), jnp.float32)
    for offset in range(conv_weight.shape[0]):
        conv_sum = conv_sum + jnp.dot(padded[offset:offset + in_rows], conv_weight[offset], preferred_element_type=jnp.float32)
    tok_rows = in_rows // 2
    tokens = lax.optimization_barrier(jnp.max(jax.nn.gelu(conv_sum, approximate=False).reshape(tok_rows, 2, width), axis=1)).astype(jnp.bfloat16)
    normed = root_norm(tokens.astype(jnp.float32), norm_gain).astype(jnp.bfloat16)
    query_all = jnp.dot(normed, query_weight, preferred_element_type=jnp.float32).astype(jnp.bfloat16)
    key_all = jnp.dot(normed, key_weight, preferred_element_type=jnp.float32).astype(jnp.bfloat16)
    value_all = jnp.dot(normed, value_weight, preferred_element_type=jnp.float32).astype(jnp.bfloat16)
    score_scale = HD ** (-0.5)

    def one_head(operands):
        query_head, key_head, value_head = operands
        scores = jnp.dot(query_head, key_head.T, preferred_element_type=jnp.float32) * score_scale
        top_score = lax.optimization_barrier(jnp.max(scores, axis=-1, keepdims=True))
        prob_rows = jnp.exp(scores - top_score)
        denominator = lax.optimization_barrier(jnp.sum(prob_rows, axis=-1, keepdims=True))
        mixed_head = jnp.dot(prob_rows.astype(jnp.bfloat16), value_head, preferred_element_type=jnp.float32)
        return mixed_head / denominator

    def split_heads(matrix):
        return matrix.reshape(tok_rows, HEADS, HD).transpose(1, 0, 2)
    head_out = lax.map(one_head, (split_heads(query_all), split_heads(key_all), split_heads(value_all)))
    attn_out = head_out.transpose(1, 0, 2).reshape(tok_rows, HEADS * HD).astype(jnp.bfloat16)
    branch = jnp.dot(attn_out, out_weight, preferred_element_type=jnp.float32)
    attended = root_norm(branch, post_gain).astype(jnp.bfloat16)
    mixed_rows = tokens.astype(jnp.float32) + attended.astype(jnp.float32)
    pooled = lax.optimization_barrier(jnp.mean(mixed_rows.reshape(tok_rows // 16, 16, width), axis=1)).astype(jnp.bfloat16)
    left_side = jnp.dot(pooled, left_weight, preferred_element_type=jnp.float32).astype(jnp.bfloat16)
    right_side = jnp.dot(pooled, right_weight, preferred_element_type=jnp.float32).astype(jnp.bfloat16)
    blocks = 2 * N_SEQ
    row_table, col_table = np.triu_indices(blocks)
    matches = tile_ids[:, None] == jnp.arange(row_table.shape[0], dtype=jnp.int32)[None, :]
    row_block = lax.optimization_barrier(jnp.sum(jnp.where(matches, jnp.asarray(row_table, jnp.int32)[None, :], 0), axis=1)).astype(jnp.int32)
    col_block = lax.optimization_barrier(jnp.sum(jnp.where(matches, jnp.asarray(col_table, jnp.int32)[None, :], 0), axis=1)).astype(jnp.int32)
    block_len = left_side.shape[0] // blocks
    left_rows = jnp.take(left_side.reshape(blocks, block_len, -1), row_block, axis=0)
    right_rows = jnp.take(right_side.reshape(blocks, block_len, -1), col_block, axis=0)
    summed = left_rows[:, :, None, :].astype(jnp.float32) + right_rows[:, None, :, :].astype(jnp.float32)
    pair_in = jax.nn.gelu(summed, approximate=False).astype(jnp.bfloat16)
    channels = pair_weight.shape[0]
    pair_flat = jnp.dot(pair_in.reshape(-1, channels), pair_weight, preferred_element_type=jnp.float32)
    pair_tiles = pair_flat.reshape(pair_in.shape).astype(jnp.bfloat16)
    return (attended, pair_tiles)
```

```python
import functools

import jax
import jax.numpy as jnp
import numpy as np
from jax import lax
from jax.experimental import pallas as pl
from jax.experimental.pallas import tpu as pltpu
from jax.sharding import PartitionSpec as P

HEADS = 4
HD = 192
HP = 256
D = 1536
QW = 384
CIN = 768
KW = 5
BF = jnp.bfloat16
F32 = jnp.float32
VMEM = 56 * 1024 * 1024
SCALE2 = float(HD ** (-0.5) * np.log2(np.e))


def params():
    return pltpu.CompilerParams(vmem_limit_bytes=VMEM)


def cost(flops, nbytes, trans=0):
    return pl.CostEstimate(flops=flops, bytes_accessed=nbytes, transcendentals=trans)


def xor_send(x, m):
    return lax.ppermute(x, "seq", [(s, s ^ m) for s in range(16)])


def y_send(x, d):
    return lax.ppermute(x, "seq", [(s, (s + 4 * d) % 16) for s in range(16)])


def y_gather(x):
    return [x, y_send(x, 1), y_send(x, 2), y_send(x, 3)]


def xc_gather(x):
    across = xor_send(x, 2)
    return [x, xor_send(x, 1), across, xor_send(across, 1)]


def gelu(x):
    return 0.5 * x * (1.0 + lax.erf(x * np.float32(np.sqrt(0.5))))


def whole(shape):
    zeros = (0,) * len(shape)
    return pl.BlockSpec(shape, lambda *_: zeros)


def dot(a, b):
    return jnp.dot(a, b, preferred_element_type=F32)


def conv_kernel(pos, pm, p0, pp, w0, w1, w2, w3, out, wall):
    y, j = pos[0], pos[1]

    @pl.when(pl.program_id(0) == 0)
    def _():
        for d, piece in enumerate((w0, w1, w2, w3)):
            base = 192 * lax.rem(y + 4 - d, 4)
            for k in range(4):
                at = pl.multiple_of(base + 48 * (j ^ k), 16)
                for t in range(KW):
                    wall[pl.ds(pl.multiple_of(at + CIN * t, 16), 48), :] = piece[t, 48 * k : 48 * k + 48, :]

    even = dot(pm[...], wall[0:1536, :]) + dot(p0[...], wall[1536:3072, :])
    even = even + dot(pp[:, 0:CIN], wall[3072:3840, :])
    odd = dot(pm[:, CIN:], wall[0:768, :]) + dot(p0[...], wall[768:2304, :])
    odd = odd + dot(pp[...], wall[2304:3840, :])
    out[...] = jnp.maximum(gelu(even), gelu(odd)).astype(BF)


def conv(pos, pm, p0, pp, pieces):
    rows = pm.shape[0]
    tile = 256
    row_spec = pl.BlockSpec((tile, 2 * CIN), lambda i: (i, 0))
    return pl.pallas_call(
        conv_kernel,
        out_shape=jax.ShapeDtypeStruct((rows, QW), BF),
        grid=(rows // tile,),
        in_specs=[pl.BlockSpec(memory_space=pltpu.SMEM)] + [row_spec] * 3 + [whole((KW, 192, QW))] * 4,
        out_specs=pl.BlockSpec((tile, QW), lambda i: (i, 0)),
        scratch_shapes=[pltpu.VMEM((KW * CIN, QW), BF)],
        compiler_params=params(),
        cost_estimate=cost(2 * 2 * rows * KW * CIN * QW, 8_000_000, rows * 2 * QW),
        name="conv",
    )(pos, pm, p0, pp, *pieces)


def qkv_kernel(pos, t0, t1, t2, t3, gain, w0, w1, w2, w3, q_out, kv_out, wall):
    y, j = pos[0], pos[1]
    toks = (t0, t1, t2, t3)
    for d, piece in enumerate((w0, w1, w2, w3)):
        base = 384 * lax.rem(y + 4 - d, 4)
        for k in range(4):
            at = pl.multiple_of(base + 96 * (j ^ k), 16)
            wall[pl.ds(at, 96), :] = piece[96 * k : 96 * k + 96, :]
    scales = []
    for k in range(4):
        total = None
        for m in range(4):
            vals = toks[m][k ^ m].astype(F32)
            part = jnp.sum(vals * vals, axis=-1, keepdims=True)
            total = part if total is None else total + part
        scales.append(lax.rsqrt(total * np.float32(1.0 / D) + 1e-06))
    rows = t0.shape[1]
    acc = [None] * 4
    for m in range(4):
        at = pl.multiple_of(384 * (j ^ m), 128)
        g = gain[j ^ m]
        normed = [(toks[m][k ^ m].astype(F32) * scales[k] * g).astype(BF) for k in range(4)]
        part = dot(jnp.concatenate(normed, axis=0), wall[pl.ds(at, 384), :])
        acc = part if m == 0 else acc + part
    acc = acc.astype(BF)
    q_out[...] = acc[:, :HP].reshape(4, rows, HP)
    kv_out[...] = acc[:, HP:]


def qkv(pos, toks, gain, pieces):
    rows = toks[0].shape[0]
    shaped = [t.reshape(4, rows // 4, QW) for t in toks]
    return pl.pallas_call(
        qkv_kernel,
        out_shape=(
            jax.ShapeDtypeStruct((4, rows // 4, HP), BF),
            jax.ShapeDtypeStruct((rows, 2 * HD), BF),
        ),
        in_specs=[pl.BlockSpec(memory_space=pltpu.SMEM)] + [pl.BlockSpec(memory_space=pltpu.VMEM)] * 9,
        scratch_shapes=[pltpu.VMEM((D, HP + 2 * HD), BF)],
        compiler_params=params(),
        cost_estimate=cost(2 * rows * D * 640, 6_000_000, rows),
        name="qkv",
    )(pos, *shaped, gain, *pieces)


def attn_kernel(qa, qb, *rest):
    kvs, out, scores = rest[:-2], rest[-2], rest[-1]
    q = jnp.concatenate([qa[0], qb[0]], axis=0)
    span = kvs[0].shape[0]
    top = None
    for n, kv in enumerate(kvs):
        s = lax.dot_general(q, kv[:, :HP], (((1,), (1,)), ((), ())), preferred_element_type=F32)
        scores[:, n * span : (n + 1) * span] = s
        most = jnp.max(s, axis=-1, keepdims=True)
        top = most if top is None else jnp.maximum(top, most)
    total, acc = None, None
    for n, kv in enumerate(kvs):
        p = jnp.exp2((scores[:, n * span : (n + 1) * span] - top) * np.float32(SCALE2))
        part = jnp.sum(p, axis=-1, keepdims=True)
        mixed = dot(p.astype(BF), kv[:, 128:])
        total = part if n == 0 else total + part
        acc = mixed if n == 0 else acc + mixed
    out[0] = (acc / total).astype(BF)


def attention(qa, qb, kvs):
    half = qa.shape[1]
    q_spec = pl.BlockSpec((1, half, HP), lambda i: (i, 0, 0))
    span = kvs[0].shape[0]
    keys = span * len(kvs)
    return pl.pallas_call(
        attn_kernel,
        out_shape=jax.ShapeDtypeStruct((4, 2 * half, HP), BF),
        grid=(4,),
        in_specs=[q_spec, q_spec] + [whole((span, 2 * HD))] * len(kvs),
        out_specs=pl.BlockSpec((1, 2 * half, HP), lambda i: (i, 0, 0)),
        scratch_shapes=[pltpu.VMEM((2 * half, keys), F32)],
        compiler_params=params(),
        cost_estimate=cost(4 * 8 * half * keys * HP, 5_000_000, 8 * half * keys),
        name="attention",
    )(qa, qb, *kvs)


def out_kernel(pos, o0, o1, o2, o3, w, gain, ta, tb, lr, att_out, lr_out):
    j = pos[1]
    branch = None
    for m, o in enumerate((o0, o1, o2, o3)):
        at = pl.multiple_of(192 * (j ^ m), 16)
        part = dot(o[:, HP - HD :], w[pl.ds(at, HD), :])
        branch = part if m == 0 else branch + part
    scale = lax.rsqrt(jnp.mean(branch * branch, axis=-1, keepdims=True) + 1e-06)
    att = (branch * scale * gain[...]).astype(BF)
    att_out[...] = att
    rows = att.shape[0]
    r = lax.broadcasted_iota(jnp.int32, (rows // 16, rows), 0)
    c = lax.broadcasted_iota(jnp.int32, (rows // 16, rows), 1)
    pool = jnp.where(c // 16 == r, 1.0 / 16.0, 0.0).astype(BF)
    half = rows // 2
    sides = None
    for m in range(4):
        at = pl.multiple_of(QW * (j ^ m), 128)
        pooled = dot(pool[:, :half], ta[m]) + dot(pool[:, half:], tb[m])
        pooled = pooled + dot(pool, att_out[:, pl.ds(at, QW)])
        part = dot(pooled.astype(BF), lr[pl.ds(at, QW), :])
        sides = part if m == 0 else sides + part
    lr_out[...] = sides.astype(BF)


def out_project(pos, os, w, gain, ta, tb, lr):
    rows = os[0].shape[0]
    return pl.pallas_call(
        out_kernel,
        out_shape=(
            jax.ShapeDtypeStruct((rows, D), BF),
            jax.ShapeDtypeStruct((rows // 16, 256), BF),
        ),
        in_specs=[pl.BlockSpec(memory_space=pltpu.SMEM)] + [pl.BlockSpec(memory_space=pltpu.VMEM)] * 9,
        compiler_params=params(),
        cost_estimate=cost(2 * rows * HEADS * HD * D, 5_000_000, rows),
        name="out_project",
    )(pos, *os, w, gain, ta, tb, lr)


def shards(
    encoder_in,
    conv_weight,
    norm_gain,
    query_weight,
    key_weight,
    value_weight,
    out_weight,
    post_gain,
    left_weight,
    right_weight,
    pair_weight,
    tile_ids,
):
    seq = lax.axis_index("seq")
    y, j = seq // 4, seq % 4
    pos = jnp.stack([y, j]).astype(jnp.int32)

    quarters = conv_weight.reshape(KW, 48, 4, QW)
    own = [lax.dynamic_index_in_dim(quarters, j ^ k, 2, keepdims=False) for k in range(4)]
    unit = jnp.concatenate([own[0]] + [xor_send(own[k], k) for k in (1, 2, 3)], axis=1)
    conv_pieces = y_gather(unit)

    ends = 15
    left = lax.ppermute(encoder_in[-2:], "seq", [(i, i + 1) for i in range(ends)])
    right = lax.ppermute(encoder_in[:2], "seq", [(i + 1, i) for i in range(ends)])
    tok = encoder_in.shape[0] // 2
    pairs = jnp.concatenate([left, encoder_in, right], axis=0).reshape(tok + 2, 2 * CIN)
    blocks = xc_gather(pairs)
    half = tok // 2

    def windows(part):
        return [
            jnp.concatenate([b[part * half + o : part * half + o + half] for b in blocks], axis=0)
            for o in range(3)
        ]

    def head_columns(k):
        def cut(w):
            return lax.dynamic_index_in_dim(w.reshape(96, HEADS, HD), j ^ k, 1, keepdims=False)

        return jnp.concatenate(
            [cut(query_weight), jnp.zeros((96, HP - HD), BF), cut(key_weight), cut(value_weight)], axis=1
        )

    heads = [head_columns(k) for k in range(4)]
    heads, conv_pieces = lax.optimization_barrier((heads, conv_pieces))
    qkv_unit = jnp.concatenate([heads[0]] + [xor_send(heads[k], k) for k in (1, 2, 3)], axis=0)
    qkv_pieces = y_gather(qkv_unit)

    pair_rows = [out_weight, xor_send(out_weight, 2)]
    pair_rows, qkv_dep = lax.optimization_barrier((jnp.stack(pair_rows), qkv_pieces))
    mine = jnp.stack(y_gather(pair_rows))
    theirs = xor_send(mine, 1)
    both = jnp.stack([mine, theirs], axis=2).reshape(4, 4, 48, D)
    order_y = jnp.mod(y - jnp.arange(4), 4)
    order_j = jnp.bitwise_xor(j, jnp.arange(4))
    out_full = both[order_y][:, order_j].reshape(HEADS * HD, D)

    gain = norm_gain.reshape(4, 1, QW)
    toks, queries, kvs = [], [], []
    for part in range(2):
        pm, p0, pp = windows(part)
        t = conv(pos, pm, p0, pp, conv_pieces)
        pieces = xc_gather(t)
        q, kv = qkv(pos, pieces, gain, qkv_pieces)
        toks.append(jnp.stack([pieces[m].reshape(4, half, QW)[m] for m in range(4)]))
        queries.append(q)
        kvs += y_gather(kv)
    mixed = attention(queries[0], queries[1], kvs)
    os = [mixed[0]] + [xor_send(mixed[k], k) for k in (1, 2, 3)]
    lr = jnp.concatenate([left_weight, right_weight], axis=1)
    attended, sides = out_project(pos, os, out_full, post_gain.reshape(1, D), toks[0], toks[1], lr)

    row = jnp.stack(xc_gather(sides))
    table = jnp.stack(y_gather(row)).reshape(32, 8, 256)

    row_table, col_table = np.triu_indices(32)
    matches = tile_ids[:, None] == jnp.arange(row_table.shape[0], dtype=jnp.int32)[None, :]

    def place(number):
        block = jnp.sum(jnp.where(matches, jnp.asarray(number, jnp.int32)[None, :], 0), axis=1)
        owner = block // 2
        back = jnp.mod(y - owner // 4, 4)
        rel = jnp.bitwise_xor(j, owner % 4)
        return (back * 4 + rel) * 2 + block % 2

    left_rows = jnp.take(table[:, :, :128], place(row_table), axis=0, mode="clip")
    right_rows = jnp.take(table[:, :, 128:], place(col_table), axis=0, mode="clip")
    summed = left_rows[:, :, None, :].astype(F32) + right_rows[:, None, :, :].astype(F32)
    pair_in = jax.nn.gelu(summed, approximate=False).astype(BF)
    pair_flat = dot(pair_in.reshape(-1, pair_weight.shape[0]), pair_weight)
    pair_tiles = pair_flat.reshape(pair_in.shape).astype(BF)
    return (attended, pair_tiles)


def solution(mesh):
    in_specs = (
        P(("dp", "seq"), None),
        P(None, "seq", None),
        P(),
        P("seq", None),
        P("seq", None),
        P("seq", None),
        P("seq", None),
        P(),
        P(),
        P(),
        P(),
        P(("dp", "seq")),
    )
    out_specs = (P(("dp", "seq"), None), P(("dp", "seq"), None, None, None))
    return jax.shard_map(shards, mesh=mesh, in_specs=in_specs, out_specs=out_specs, check_vma=False)
```

```python
import functools

import jax
import jax.numpy as jnp
import numpy as np
from jax import lax
from jax.experimental import pallas as pl
from jax.experimental.pallas import tpu as pltpu
from jax.sharding import PartitionSpec as P

HEADS = 4
HD = 192
HP = 256
D = 1536
QW = 384
CIN = 768
KW = 5
BF = jnp.bfloat16
F32 = jnp.float32
SCALE2 = float(HD ** (-0.5) * np.log2(np.e))


def params(mib):
    return pltpu.CompilerParams(vmem_limit_bytes=mib * 1024 * 1024)


def cost(flops, nbytes, trans=0):
    return pl.CostEstimate(flops=flops, bytes_accessed=nbytes, transcendentals=trans)


def xor_send(x, m):
    return lax.ppermute(x, "seq", [(s, s ^ m) for s in range(16)])


def y_send(x, d):
    return lax.ppermute(x, "seq", [(s, (s + 4 * d) % 16) for s in range(16)])


def tie(x, *others):
    return lax.optimization_barrier((x,) + others)[0]


def xc_gather(x):
    across = xor_send(x, 2)
    return [x, xor_send(x, 1), across, xor_send(across, 1)]


def gelu(x):
    return 0.5 * x * (1.0 + lax.erf(x * np.float32(np.sqrt(0.5))))


def whole(shape):
    zeros = (0,) * len(shape)
    return pl.BlockSpec(shape, lambda *_: zeros)


def dot(a, b):
    return jnp.dot(a, b, preferred_element_type=F32)


def vmem():
    return pl.BlockSpec(memory_space=pltpu.VMEM)


def smem():
    return pl.BlockSpec(memory_space=pltpu.SMEM)


MSG_EDGE, MSG = 240, 256
X_HEAD, X_DIAG, X_ALL = 256, 304, 352
W_EDGE, W_ALL = 960, 1024
P_Q, P_OUT, P_ALL, P_HALF = 384, 576, 768, 384


def message_kernel(pos, w, rows, o0, o1, o2, o3, w_in, ends, sems):
    copies = [pltpu.make_async_copy(w.at[t], w_in.at[t], sems.at[t]) for t in range(KW)]
    last = rows.shape[0] - 16
    copies.append(pltpu.make_async_copy(rows.at[pl.ds(0, 16)], ends.at[0], sems.at[KW]))
    copies.append(pltpu.make_async_copy(rows.at[pl.ds(last, 16)], ends.at[1], sems.at[KW + 1]))
    for copy in copies:
        copy.start()
    for copy in copies:
        copy.wait()
    at = lax.broadcasted_iota(jnp.int32, (16, QW), 0)
    edges = jnp.zeros((16, QW), F32)
    first, final = ends[0].astype(F32), ends[1].astype(F32)
    lines = [first[0:1], first[1:2], final[14:15], final[15:16]]
    for n in range(8):
        edges = jnp.where(at == n, lines[n // 2][:, (n % 2) * QW : (n % 2) * QW + QW], edges)
    edges = edges.astype(BF)
    for k, out in enumerate((o0, o1, o2, o3)):
        cols = pl.ds(pl.multiple_of(QW * (pos[1] ^ k), 128), QW)
        for t in range(KW):
            out[48 * t : 48 * t + 48, :] = w_in[t, :, cols]
        out[MSG_EDGE:MSG, :] = edges


def hbm():
    return pl.BlockSpec(memory_space=pltpu.HBM)


def messages(pos, w, rows):
    return pl.pallas_call(
        message_kernel,
        out_shape=[jax.ShapeDtypeStruct((MSG, QW), BF)] * 4,
        in_specs=[smem(), hbm(), hbm()],
        out_specs=[vmem()] * 4,
        scratch_shapes=[
            pltpu.VMEM((KW, 48, D), BF),
            pltpu.VMEM((2, 16, CIN), BF),
            pltpu.SemaphoreType.DMA((KW + 2,)),
        ],
        compiler_params=params(56),
        cost_estimate=cost(0, 3_000_000),
        name="messages",
    )(pos, w, rows)


def row_message_kernel(pos, pairs, wq, wk, wv, near, far, own):
    near[0:X_HEAD, :] = pairs[...]
    far[0:X_HEAD, :] = pairs[...]
    for place in range(4):

        @pl.when(pos[1] == place)
        def _():
            for k, (out, at) in enumerate(((own, 0), (near, X_HEAD), (far, X_HEAD), (far, X_DIAG))):
                cols = slice(HD * (place ^ k), HD * (place ^ k) + HD)
                keys, values, queries = wk[:, cols], wv[:, cols], wq[:, cols]
                both = jnp.concatenate([keys, values], axis=1)
                out[at : at + 48, 0:QW] = both[0:48]
                out[at : at + 48, QW : 2 * QW] = both[48:96]
                out[at : at + 48, 2 * QW : 3 * QW] = jnp.concatenate([queries[0:48], queries[48:96]], axis=1)
                out[at : at + 48, 3 * QW :] = jnp.zeros((48, QW), BF)


def row_messages(pos, pairs, wq, wk, wv):
    return pl.pallas_call(
        row_message_kernel,
        out_shape=[jax.ShapeDtypeStruct((r, 2 * CIN), BF) for r in (X_DIAG, X_ALL, 48)],
        in_specs=[smem()] + [vmem()] * 4,
        out_specs=[vmem()] * 3,
        compiler_params=params(8),
        cost_estimate=cost(0, 4_000_000),
        name="row_messages",
    )(pos, pairs, wq, wk, wv)


def w_unit_kernel(pos, m0, m1, m2, m3, out):
    for k, m in enumerate((m0, m1, m2, m3)):
        j = pos[1] ^ k
        for t in range(KW):
            out[pl.ds(pl.multiple_of(192 * t + 48 * j, 16), 48), :] = m[48 * t : 48 * t + 48, :]
        out[pl.ds(pl.multiple_of(W_EDGE + 16 * j, 16), 16), :] = m[MSG_EDGE:MSG, :]


def w_unit(pos, msgs):
    return pl.pallas_call(
        w_unit_kernel,
        out_shape=jax.ShapeDtypeStruct((W_ALL, QW), BF),
        in_specs=[smem()] + [vmem()] * 4,
        out_specs=vmem(),
        compiler_params=params(8),
        cost_estimate=cost(0, 1_500_000),
        name="w_unit",
    )(pos, *msgs)


def p_unit_kernel(pos, x0, x1, x2, x3, wo, out):
    for c in range(4):
        out[P_OUT + 48 * c : P_OUT + 48 * c + 48, :] = wo[:, QW * c : QW * c + QW]
    for k, (x, at) in enumerate(((x0, 0), (x1, X_HEAD), (x2, X_HEAD), (x3, X_DIAG))):
        j = pos[1] ^ k
        for n in range(2):
            rows = pl.ds(pl.multiple_of(96 * j + 48 * n, 16), 48)
            out[rows, :] = x[at : at + 48, QW * n : QW * n + QW]
        out[pl.ds(pl.multiple_of(P_Q + 48 * j, 16), 48), :] = x[at : at + 48, 2 * QW : 3 * QW]


def p_unit(pos, parts, wo):
    return pl.pallas_call(
        p_unit_kernel,
        out_shape=jax.ShapeDtypeStruct((P_ALL, QW), BF),
        in_specs=[smem()] + [vmem()] * 5,
        out_specs=vmem(),
        compiler_params=params(8),
        cost_estimate=cost(0, 1_000_000),
        name="p_unit",
    )(pos, *parts, wo)


def halves_kernel(one, three, low, high):
    cut = low.shape[0]
    low[...] = one[0:cut, :]
    high[...] = three[cut : 2 * cut, :]


def halves(one, three, cut):
    return pl.pallas_call(
        halves_kernel,
        out_shape=[jax.ShapeDtypeStruct((cut, QW), BF)] * 2,
        in_specs=[vmem()] * 2,
        out_specs=[vmem()] * 2,
        compiler_params=params(8),
        cost_estimate=cost(0, 1_000_000),
        name="halves",
    )(one, three)


def conv_kernel(pos, b0, b1, b2, b3, w0, w1, w3, w2_low, w2_high, out, wall, before, after):
    y, j = pos[0], pos[1]

    def place(back, tap, channel, rows):
        at = CIN * tap + 192 * lax.rem(y + 4 - back, 4) + channel
        wall[pl.ds(pl.multiple_of(at, 16), rows.shape[0]), :] = rows

    for back, piece in ((0, w0), (1, w1), (3, w3)):
        for t in range(KW):
            place(back, t, 0, piece[192 * t : 192 * t + 192, :])
    for t in range(2):
        place(2, t, 0, w2_low[192 * t : 192 * t + 192, :])
        place(2, 3 + t, 0, w2_high[96 + 192 * t : 96 + 192 * t + 192, :])
    place(2, 2, 0, w2_low[384:480, :])
    place(2, 2, 96, w2_high[0:96, :])

    blocks = (b0, b1, b2, b3)
    at = lax.broadcasted_iota(jnp.int32, (16, 2 * CIN), 0)

    def edge(ref, first_row, line, at_row, there):
        rows = ref[first_row : first_row + 16, :].astype(F32)
        joined = jnp.concatenate([rows[line + n : line + n + 1] for n in range(4)], axis=1)
        return jnp.where((at == at_row) & there, joined, 0.0).astype(BF)

    before[0:16, :] = edge(w1, W_EDGE + 48, 4, 15, y > 0)
    after[64:80, :] = edge(w3, W_EDGE, 0, 0, y < 3)
    for k in range(4):
        before[pl.ds(pl.multiple_of(16 * ((j ^ k) + 1), 16), 16), :] = blocks[k][X_HEAD - 16 : X_HEAD, :]
        after[pl.ds(pl.multiple_of(16 * (j ^ k), 16), 16), :] = blocks[k][0:16, :]
    tile = X_HEAD // 2
    for n in range(8):
        k, part = n // 2, n % 2
        block = blocks[k]
        if part == 0:
            beside = before[pl.ds(pl.multiple_of(16 * (j ^ k), 16), 16), :]
            near = jnp.concatenate([beside, block[0 : tile + 16, :]], axis=0)
        else:
            beside = after[pl.ds(pl.multiple_of(16 * ((j ^ k) + 1), 16), 16), :]
            near = jnp.concatenate([block[tile - 16 : X_HEAD, :], beside], axis=0)
        pm, p0, pp = near[15 : tile + 15], near[16 : tile + 16], near[17 : tile + 17]
        even = dot(pm, wall[0:1536, :]) + dot(p0, wall[1536:3072, :])
        even = even + dot(pp[:, 0:CIN], wall[3072:3840, :])
        odd = dot(pm[:, CIN:], wall[0:768, :]) + dot(p0, wall[768:2304, :])
        odd = odd + dot(pp, wall[2304:3840, :])
        out[n * tile : (n + 1) * tile, :] = jnp.maximum(gelu(even), gelu(odd)).astype(BF)


def conv(pos, blocks, pieces):
    rows = 4 * X_HEAD
    return pl.pallas_call(
        conv_kernel,
        out_shape=jax.ShapeDtypeStruct((rows, QW), BF),
        in_specs=[smem()] + [vmem()] * 9,
        out_specs=vmem(),
        scratch_shapes=[pltpu.VMEM((KW * CIN, QW), BF)] + [pltpu.VMEM((80, 2 * CIN), BF)] * 2,
        compiler_params=params(12),
        cost_estimate=cost(2 * 2 * rows * KW * CIN * QW, 8_000_000, rows * 2 * QW),
        name="conv",
    )(pos, *blocks, *pieces)


def qkv_kernel(pos, t0, t1, t2, t3, gain, w0, w1, w3, low, high, q_out, kv_out, wall):
    y, j = pos[0], pos[1]
    toks = (t0, t1, t2, t3)
    gap = jnp.zeros((48, HP - HD), BF)
    for back, kv, piece, q_at in ((0, w0, w0, P_Q), (1, w1, w1, P_Q), (3, w3, w3, P_Q), (2, low, high, 0)):
        base = 384 * lax.rem(y + 4 - back, 4)
        wall[pl.ds(pl.multiple_of(base, 128), 384), HP:] = kv[0:P_Q, :]
        for n in range(4):
            for side in range(2):
                rows = piece[q_at + 48 * n : q_at + 48 * n + 48, HD * side : HD * side + HD]
                at = pl.multiple_of(base + 96 * n + 48 * side, 16)
                wall[pl.ds(at, 48), 0:HP] = jnp.concatenate([rows, gap], axis=1)
    scales = []
    for k in range(4):
        total = None
        for m in range(4):
            vals = toks[m][k ^ m].astype(F32)
            part = jnp.sum(vals * vals, axis=-1, keepdims=True)
            total = part if total is None else total + part
        scales.append(lax.rsqrt(total * np.float32(1.0 / D) + 1e-06))
    rows = t0.shape[1]
    acc = [None] * 4
    for m in range(4):
        at = pl.multiple_of(384 * (j ^ m), 128)
        g = gain[j ^ m]
        normed = [(toks[m][k ^ m].astype(F32) * scales[k] * g).astype(BF) for k in range(4)]
        part = dot(jnp.concatenate(normed, axis=0), wall[pl.ds(at, 384), :])
        acc = part if m == 0 else acc + part
    acc = acc.astype(BF)
    q_out[...] = acc[:, :HP].reshape(4, rows, HP)
    kv_out[...] = acc[:, HP:]


def qkv(pos, toks, gain, pieces):
    rows = toks[0].shape[0]
    shaped = [t.reshape(4, rows // 4, QW) for t in toks]
    return pl.pallas_call(
        qkv_kernel,
        out_shape=(
            jax.ShapeDtypeStruct((4, rows // 4, HP), BF),
            jax.ShapeDtypeStruct((rows, 2 * HD), BF),
        ),
        in_specs=[smem()] + [vmem()] * 10,
        out_specs=(vmem(), vmem()),
        scratch_shapes=[pltpu.VMEM((D, HP + 2 * HD), BF)],
        compiler_params=params(20),
        cost_estimate=cost(2 * rows * D * 640, 6_000_000, rows),
        name="qkv",
    )(pos, *shaped, gain, *pieces)


def attn_kernel(merge, last, n_kv, *refs):
    kvs = refs[1 : 1 + n_kv]
    rest = refs[1 + n_kv :]
    if merge:
        acc_in, top_in, sum_in = rest[:3]
    scores = rest[-1]
    q = refs[0][0]
    top, at = None, 0
    spans = []
    for kv in kvs:
        n = kv.shape[0] // 128 * 128
        s = lax.dot_general(q, kv[0:n, :HP], (((1,), (1,)), ((), ())), preferred_element_type=F32)
        scores[:, at : at + n] = s
        most = jnp.max(s, axis=-1, keepdims=True)
        top = most if top is None else jnp.maximum(top, most)
        spans.append((kv, at, n))
        at += n
    if merge:
        top = jnp.maximum(top, top_in[0])
        fade = jnp.exp2((top_in[0] - top) * np.float32(SCALE2))
        total, acc = sum_in[0] * fade, acc_in[0] * fade
    else:
        total, acc = 0.0, 0.0
    for kv, at, n in spans:
        p = jnp.exp2((scores[:, at : at + n] - top) * np.float32(SCALE2))
        total = total + jnp.sum(p, axis=-1, keepdims=True)
        acc = acc + dot(p.astype(BF), kv[0:n, 128:])
    if last:
        rest[-2][0] = (acc / total).astype(BF)
    else:
        out, top_out, sum_out = rest[-4:-1]
        out[0] = acc
        top_out[0] = top
        sum_out[0] = total


def attention(q, kvs, before=None, last=False):
    rows = q.shape[1]
    keys = sum(kv.shape[0] // 128 * 128 for kv in kvs)

    def spec(r, c):
        return pl.BlockSpec((1, r, c), lambda i: (i, 0, 0))

    state = [spec(rows, c) for c in (HP, 1, 1)]
    shapes = [jax.ShapeDtypeStruct((4, rows, c), F32) for c in (HP, 1, 1)]
    return pl.pallas_call(
        functools.partial(attn_kernel, before is not None, last, len(kvs)),
        out_shape=jax.ShapeDtypeStruct((4, rows, HP), BF) if last else shapes,
        grid=(4,),
        in_specs=[spec(rows, HP)] + [whole(kv.shape) for kv in kvs] + (state if before else []),
        out_specs=spec(rows, HP) if last else state,
        scratch_shapes=[pltpu.VMEM((rows, keys), F32)],
        compiler_params=params(14),
        cost_estimate=cost(4 * 4 * rows * keys * HP, 5_000_000, 4 * rows * keys),
        name="attention",
    )(q, *kvs, *(before or ()))


def out_kernel(pos, o0, o1, o2, o3, b0, b1, b2, b3, gain, toks, lr, att_out, lr_out, w):
    y, j = pos[0], pos[1]
    for k, block in enumerate((b0, b1, b2, b3)):
        for n, back in enumerate((0, 1, 3, 2)):
            at = pl.multiple_of(HD * lax.rem(y + 4 - back, 4) + 48 * (j ^ k), 16)
            for c in range(4):
                w[pl.ds(at, 48), QW * c : QW * c + QW] = block[n, 48 * c : 48 * c + 48, :]
    branch = None
    for m, o in enumerate((o0, o1, o2, o3)):
        at = pl.multiple_of(192 * (j ^ m), 16)
        part = dot(o[:, HP - HD :], w[pl.ds(at, HD), :])
        branch = part if m == 0 else branch + part
    scale = lax.rsqrt(jnp.mean(branch * branch, axis=-1, keepdims=True) + 1e-06)
    att = (branch * scale * gain[...]).astype(BF)
    att_out[...] = att
    rows = att.shape[0]
    r = lax.broadcasted_iota(jnp.int32, (rows // 16, rows), 0)
    c = lax.broadcasted_iota(jnp.int32, (rows // 16, rows), 1)
    pool = jnp.where(c // 16 == r, 1.0 / 16.0, 0.0).astype(BF)
    sides = None
    for m in range(4):
        at = pl.multiple_of(QW * (j ^ m), 128)
        pooled = dot(pool, toks[m]) + dot(pool, att_out[:, pl.ds(at, QW)])
        part = dot(pooled.astype(BF), lr[pl.ds(at, QW), :])
        sides = part if m == 0 else sides + part
    lr_out[...] = sides.astype(BF)


def out_project(pos, os, blocks, gain, toks, lr):
    rows = os[0].shape[0]
    return pl.pallas_call(
        out_kernel,
        out_shape=(
            jax.ShapeDtypeStruct((rows, D), BF),
            jax.ShapeDtypeStruct((rows // 16, 256), BF),
        ),
        in_specs=[smem()] + [vmem()] * 11,
        out_specs=(vmem(), vmem()),
        scratch_shapes=[pltpu.VMEM((HEADS * HD, D), BF)],
        compiler_params=params(12),
        cost_estimate=cost(2 * rows * HEADS * HD * D, 5_000_000, rows),
        name="out_project",
    )(pos, *os, *blocks, gain, toks, lr)


def pair_kernel(rows, cols, r0, r1, r2, r3, w, out, table, mixed):
    for d, r in enumerate((r0, r1, r2, r3)):
        table[8 * d : 8 * d + 8] = r[...].astype(F32).reshape(8, 8, 256)
    tiles = out.shape[0]
    for t in range(tiles):
        left = table[rows[t]][:, :128]
        right = table[cols[t]][:, 128:]
        z = gelu(left[:, None, :] + right[None, :, :])
        mixed[64 * t : 64 * t + 64, :] = z.reshape(64, 128).astype(BF)
    out[...] = dot(mixed[...], w[...]).reshape(tiles, 8, 8, 128).astype(BF)


def pair(rows, cols, sides, w):
    tiles = rows.shape[0]
    return pl.pallas_call(
        pair_kernel,
        out_shape=jax.ShapeDtypeStruct((tiles, 8, 8, 128), BF),
        in_specs=[smem()] * 2 + [vmem()] * 5,
        out_specs=vmem(),
        scratch_shapes=[pltpu.VMEM((32, 8, 256), F32), pltpu.VMEM((tiles * 64, 128), BF)],
        compiler_params=params(8),
        cost_estimate=cost(2 * tiles * 64 * 128 * 128, 1_000_000, tiles * 64 * 128),
        name="pair",
    )(rows, cols, *sides, w)


def shards(
    encoder_in,
    conv_weight,
    norm_gain,
    query_weight,
    key_weight,
    value_weight,
    out_weight,
    post_gain,
    left_weight,
    right_weight,
    pair_weight,
    tile_ids,
):
    seq = lax.axis_index("seq")
    y, j = seq // 4, seq % 4
    pos = jnp.stack([y, j]).astype(jnp.int32)

    msgs = messages(pos, conv_weight, encoder_in)
    msgs = [msgs[0]] + [xor_send(msgs[k], k) for k in (1, 2, 3)]
    w_own = w_unit(pos, msgs)
    w_one, w_three = y_send(w_own, 1), y_send(w_own, 3)

    tok = encoder_in.shape[0] // 2
    pairs = encoder_in.reshape(tok, 2 * CIN)
    near, far, head = row_messages(pos, pairs, query_weight, key_weight, value_weight)
    far = tie(far, w_own)
    w_low, w_high = halves(w_one, w_three, 480)
    across, near, w_low, w_high = lax.optimization_barrier((xor_send(far, 2), near, w_low, w_high))
    beside, diagonal = xor_send(near, 1), xor_send(across, 1)
    blocks = [pairs, beside, across, diagonal]
    p_own = p_unit(pos, [head, beside, across, diagonal], out_weight)

    w_pieces = [w_own, w_one, w_three, y_send(w_low, 1), y_send(w_high, 3)]
    p_own = tie(p_own, w_low)
    p_one, p_three = y_send(p_own, 1), y_send(p_own, 3)

    gain = norm_gain.reshape(4, 1, QW)
    tok_own, p_one, p_three = lax.optimization_barrier((conv(pos, blocks, w_pieces), p_one, p_three))
    low, high = halves(p_one, p_three, P_HALF)
    low, high = y_send(low, 1), y_send(high, 3)
    tok_across, low, high = lax.optimization_barrier((xor_send(tok_own, 2), low, high))
    tokens = [tok_own, xor_send(tok_own, 1), tok_across, xor_send(tok_across, 1)]
    q, kv = qkv(pos, tokens, gain, [p_own, p_one, p_three, low, high])
    out_rows = [p_own[P_OUT:], p_one[P_OUT:], p_three[P_OUT:], high[P_OUT - P_HALF :]]
    one, three = y_send(kv, 1), y_send(kv, 3)
    cut = kv.shape[0] // 2
    low, high = halves(one, three, cut)
    low, high = y_send(low, 1), y_send(high, 3)
    out_rows = jnp.stack(tie(out_rows, kv))
    out_across = xor_send(out_rows, 2)
    state = attention(q, [kv, one, three])
    out_across, out_own = tie((out_across, out_rows), state)
    out_blocks = [out_rows, xor_send(out_own, 1), out_across, xor_send(out_across, 1)]
    mixed = attention(q, [low, high], state, True)
    os = [mixed[0]] + [xor_send(mixed[k], k) for k in (1, 2, 3)]

    own_tokens = jnp.stack([tokens[m].reshape(4, tok, QW)[m] for m in range(4)])
    lr = jnp.concatenate([left_weight, right_weight], axis=1)
    attended, sides = out_project(pos, os, out_blocks, post_gain.reshape(1, D), own_tokens, lr)

    row = jnp.stack([sides] + [xor_send(sides, k) for k in (1, 2, 3)])
    rows_all = [row] + [y_send(row, d) for d in (1, 2, 3)]

    row_table, col_table = np.triu_indices(32)
    matches = tile_ids[:, None] == jnp.arange(row_table.shape[0], dtype=jnp.int32)[None, :]

    def place(number):
        block = jnp.sum(jnp.where(matches, jnp.asarray(number, jnp.int32)[None, :], 0), axis=1)
        owner = block // 2
        back = jnp.mod(y - owner // 4, 4)
        rel = jnp.bitwise_xor(j, owner % 4)
        return (back * 4 + rel) * 2 + block % 2

    pair_tiles = pair(place(row_table), place(col_table), rows_all, pair_weight)
    return (attended, pair_tiles)


def solution(mesh):
    in_specs = (
        P(("dp", "seq"), None),
        P(None, "seq", None),
        P(),
        P("seq", None),
        P("seq", None),
        P("seq", None),
        P("seq", None),
        P(),
        P(),
        P(),
        P(),
        P(("dp", "seq")),
    )
    out_specs = (P(("dp", "seq"), None), P(("dp", "seq"), None, None, None))
    return jax.shard_map(shards, mesh=mesh, in_specs=in_specs, out_specs=out_specs, check_vma=False)
```

```python
import functools

import jax
import jax.numpy as jnp
import numpy as np
from jax import lax
from jax.experimental import pallas as pl
from jax.experimental.pallas import tpu as pltpu
from jax.sharding import PartitionSpec as P

HEADS = 4
BLOCK = 256
HD = 192
HP = 256
D = 1536
QW = 384
CIN = 768
KW = 5
BF = jnp.bfloat16
F32 = jnp.float32
SCALE2 = float(HD ** (-0.5) * np.log2(np.e))


def params(mib):
    return pltpu.CompilerParams(vmem_limit_bytes=mib * 1024 * 1024)


def cost(flops, nbytes, trans=0):
    return pl.CostEstimate(flops=flops, bytes_accessed=nbytes, transcendentals=trans)


def xor_send(x, m):
    return lax.ppermute(x, "seq", [(s, s ^ m) for s in range(16)])


def y_send(x, d):
    return lax.ppermute(x, "seq", [(s, (s + 4 * d) % 16) for s in range(16)])


def tie(x, *others):
    return lax.optimization_barrier((x,) + others)[0]


def gelu(x):
    return 0.5 * x * (1.0 + lax.erf(x * np.float32(np.sqrt(0.5))))


def whole(shape):
    zeros = (0,) * len(shape)
    return pl.BlockSpec(shape, lambda *_: zeros)


def dot(a, b):
    return jnp.dot(a, b, preferred_element_type=F32)


def vmem():
    return pl.BlockSpec(memory_space=pltpu.VMEM)


def smem():
    return pl.BlockSpec(memory_space=pltpu.SMEM)


MSG_EDGE, MSG_KV, MSG_Q, MSG = 240, 256, 352, 400
W_EDGE, W_ALL = 960, 1024
HEAD_ROWS = MSG - MSG_KV


def message_kernel(pos, w, rows, wq, wk, wv, o0, o1, o2, o3, w_in, ends, q_in, k_in, v_in, sems):
    copies = [pltpu.make_async_copy(w.at[t], w_in.at[t], sems.at[t]) for t in range(KW)]
    last = rows.shape[0] - 16
    copies.append(pltpu.make_async_copy(rows.at[pl.ds(0, 16)], ends.at[0], sems.at[KW]))
    copies.append(pltpu.make_async_copy(rows.at[pl.ds(last, 16)], ends.at[1], sems.at[KW + 1]))
    for n, (src, dst) in enumerate(((wq, q_in), (wk, k_in), (wv, v_in))):
        copies.append(pltpu.make_async_copy(src, dst, sems.at[KW + 2 + n]))
    for copy in copies:
        copy.start()
    for copy in copies:
        copy.wait()
    at = lax.broadcasted_iota(jnp.int32, (16, QW), 0)
    edges = jnp.zeros((16, QW), F32)
    first, final = ends[0].astype(F32), ends[1].astype(F32)
    lines = [first[0:1], first[1:2], final[14:15], final[15:16]]
    for n in range(8):
        edges = jnp.where(at == n, lines[n // 2][:, (n % 2) * QW : (n % 2) * QW + QW], edges)
    edges = edges.astype(BF)
    outs = (o0, o1, o2, o3)
    for d, out in enumerate(outs):
        cols = pl.ds(pl.multiple_of(QW * lax.rem(pos[0] + d, 4), 128), QW)
        for t in range(KW):
            out[48 * t : 48 * t + 48, :] = w_in[t, :, cols]
        out[MSG_EDGE:MSG_KV, :] = edges
    for place in range(4):

        @pl.when(pos[0] == place)
        def _():
            for d, out in enumerate(outs):
                head = (place + d) % 4
                cols = slice(HD * head, HD * head + HD)
                out[MSG_KV:MSG_Q, :] = jnp.concatenate([k_in[:, cols], v_in[:, cols]], axis=1)
                out[MSG_Q:MSG, :] = jnp.concatenate([q_in[0:48, cols], q_in[48:96, cols]], axis=1)


def hbm():
    return pl.BlockSpec(memory_space=pltpu.HBM)


def messages(pos, w, rows, wq, wk, wv):
    return pl.pallas_call(
        message_kernel,
        out_shape=[jax.ShapeDtypeStruct((MSG, QW), BF)] * 4,
        in_specs=[smem()] + [hbm()] * 5,
        out_specs=[vmem()] * 4,
        scratch_shapes=[pltpu.VMEM((KW, 48, D), BF), pltpu.VMEM((2, 16, CIN), BF)]
        + [pltpu.VMEM((96, HEADS * HD), BF)] * 3
        + [pltpu.SemaphoreType.DMA((KW + 5,))],
        compiler_params=params(56),
        cost_estimate=cost(0, 3_000_000),
        name="messages",
    )(pos, w, rows, wq, wk, wv)


def unit_kernel(m0, m1, m2, m3, w_out, p_out):
    for d, m in enumerate((m0, m1, m2, m3)):
        w_out[MSG_EDGE * d : MSG_EDGE * d + MSG_EDGE, :] = m[0:MSG_EDGE, :]
        w_out[W_EDGE + 16 * d : W_EDGE + 16 * d + 16, :] = m[MSG_EDGE:MSG_KV, :]
        p_out[HEAD_ROWS * d : HEAD_ROWS * d + HEAD_ROWS, :] = m[MSG_KV:MSG, :]


def units(msgs):
    return pl.pallas_call(
        unit_kernel,
        out_shape=[jax.ShapeDtypeStruct((r, QW), BF) for r in (W_ALL, 4 * HEAD_ROWS)],
        in_specs=[vmem()] * 4,
        out_specs=[vmem()] * 2,
        compiler_params=params(8),
        cost_estimate=cost(0, 1_500_000),
        name="units",
    )(*msgs)


def halves_kernel(one, three, low, high):
    cut = low.shape[0]
    low[...] = one[0:cut, :]
    high[...] = three[cut : 2 * cut, :]


def halves(one, three, cut):
    return pl.pallas_call(
        halves_kernel,
        out_shape=[jax.ShapeDtypeStruct((cut, one.shape[1]), BF)] * 2,
        in_specs=[vmem()] * 2,
        out_specs=[vmem()] * 2,
        compiler_params=params(8),
        cost_estimate=cost(0, 1_000_000),
        name="halves",
    )(one, three)


def place_weights(pos, unit_refs, wall, edges):
    y, g = pos[0], pos[1]
    edges[0:16, :] = jnp.zeros((16, QW), BF)
    edges[272:288, :] = jnp.zeros((16, QW), BF)
    for k, unit in enumerate(unit_refs):
        for back in range(4):
            device = 4 * lax.rem(y + 4 - back, 4) + (g ^ k)
            at = pl.multiple_of(48 * device, 16)
            for t in range(KW):
                start = MSG_EDGE * back + 48 * t
                wall[pl.ds(at + CIN * t, 48), :] = unit[start : start + 48, :]
            lines = W_EDGE + 16 * back
            edges[pl.ds(pl.multiple_of(16 * (device + 1), 16), 16), :] = unit[lines : lines + 16, :]


def block_tokens(device, block, wall, edges):
    at = lax.broadcasted_iota(jnp.int32, (16, 2 * CIN), 0)

    def beside(place, line, row):
        rows = edges[pl.ds(pl.multiple_of(16 * place, 16), 16), :].astype(F32)
        joined = jnp.concatenate([rows[line + n : line + n + 1] for n in range(4)], axis=1)
        return jnp.where(at == row, joined, 0.0).astype(BF)

    near = jnp.concatenate([beside(device, 4, 15), block, beside(device + 2, 0, 0)], axis=0)
    pm, p0, pp = (near[15 + n : 15 + n + BLOCK] for n in range(3))
    halves_of = [v[:, n : n + CIN] for v in (pm, p0, pp) for n in (0, CIN)]
    acc = None
    for t in range(KW):
        pair = jnp.concatenate(halves_of[t : t + 2], axis=0)
        part = dot(pair, wall[CIN * t : CIN * t + CIN, :])
        acc = part if t == 0 else acc + part
    return jnp.maximum(gelu(acc[:BLOCK]), gelu(acc[BLOCK:])).astype(BF)


def device_at(pos, back):
    return 4 * lax.rem(pos[0] + 4 - back, 4) + pos[1]


def conv_first_kernel(pos, b0, b1, b3, u0, u1, u2, u3, out, wall, edges):
    place_weights(pos, (u0, u1, u2, u3), wall, edges)
    for n, (back, block) in enumerate(((0, b0), (1, b1), (3, b3))):
        out[BLOCK * n : BLOCK * n + BLOCK, :] = block_tokens(device_at(pos, back), block[...], wall, edges)


def conv_second_kernel(pos, low, high, wall, edges, first, out):
    block = jnp.concatenate([low[...], high[...]], axis=0)
    out[0 : 2 * BLOCK, :] = first[0 : 2 * BLOCK, :]
    out[2 * BLOCK : 3 * BLOCK, :] = block_tokens(device_at(pos, 2), block, wall, edges)
    out[3 * BLOCK :, :] = first[2 * BLOCK :, :]


def conv_call(kernel, name, shapes, *operands):
    return pl.pallas_call(
        kernel,
        out_shape=[jax.ShapeDtypeStruct((r, QW), BF) for r in shapes],
        in_specs=[smem()] + [vmem()] * (len(operands) - 1),
        out_specs=[vmem()] * len(shapes),
        compiler_params=params(14),
        cost_estimate=cost(2 * 2 * BLOCK * KW * CIN * QW, 8_000_000, 4 * BLOCK * QW),
        name=name,
    )(*operands)


def qkv_kernel(pos, t0, t1, t3, low, high, gain, u0, u1, u2, u3, q_out, kv_out, wall):
    y, g = pos[0], pos[1]
    gap = jnp.zeros((48, HP - HD), BF)
    for k, unit in enumerate((u0, u1, u2, u3)):
        for back in range(4):
            at = pl.multiple_of(96 * (4 * lax.rem(y + 4 - back, 4) + (g ^ k)), 16)
            top = HEAD_ROWS * back
            wall[pl.ds(at, 96), HP:] = unit[top : top + 96, :]
            for side in range(2):
                rows = unit[top + 96 : top + 144, HD * side : HD * side + HD]
                wall[pl.ds(at + 48 * side, 48), 0:HP] = jnp.concatenate([rows, gap], axis=1)

    def tokens(back, block):
        at = (block - back) % 4
        ref = {0: t0, 1: t1, 2: (low, high)[at // 2], 3: t3}[back]
        at = at % 2 if back == 2 else at
        return ref[BLOCK * at : BLOCK * at + BLOCK, :].astype(F32)

    for block in range(4):
        squares = 0.0
        for back in range(4):
            vals = tokens(back, block)
            squares = squares + jnp.sum(vals * vals, axis=-1, keepdims=True)
        scale = lax.rsqrt(squares * np.float32(1.0 / D) + 1e-06)
        acc = 0.0
        for back in range(4):
            place = lax.rem(y + 4 - back, 4)
            normed = (tokens(back, block) * scale * gain[place]).astype(BF)
            acc = acc + dot(normed, wall[pl.ds(pl.multiple_of(QW * place, 128), QW), :])
        done = acc.astype(BF)
        q_out[block] = done[:, :HP]
        kv_out[BLOCK * block : BLOCK * block + BLOCK, :] = done[:, HP:]


def qkv(pos, tokens, gain, head_units):
    rows = tokens[0].shape[0]
    return pl.pallas_call(
        qkv_kernel,
        out_shape=[jax.ShapeDtypeStruct((4, BLOCK, HP), BF), jax.ShapeDtypeStruct((rows, QW), BF)],
        in_specs=[smem()] + [vmem()] * 10,
        out_specs=[vmem()] * 2,
        scratch_shapes=[pltpu.VMEM((D, HP + QW), BF)],
        compiler_params=params(14),
        cost_estimate=cost(2 * rows * D * 640, 6_000_000, rows),
        name="qkv",
    )(pos, *tokens, gain, *head_units)


def attn_kernel(merge, last, n_kv, *refs):
    kvs = refs[1 : 1 + n_kv]
    rest = refs[1 + n_kv :]
    if merge:
        acc_in, top_in, sum_in = rest[:3]
    scores = rest[-1]
    q = refs[0][0]
    top, at = None, 0
    spans = []
    for kv in kvs:
        n = kv.shape[0] // 128 * 128
        s = lax.dot_general(q, kv[0:n, :HP], (((1,), (1,)), ((), ())), preferred_element_type=F32)
        scores[:, at : at + n] = s
        most = jnp.max(s, axis=-1, keepdims=True)
        top = most if top is None else jnp.maximum(top, most)
        spans.append((kv, at, n))
        at += n
    if merge:
        top = jnp.maximum(top, top_in[0])
        fade = jnp.exp2((top_in[0] - top) * np.float32(SCALE2))
        total, acc = sum_in[0] * fade, acc_in[0] * fade
    else:
        total, acc = 0.0, 0.0
    for kv, at, n in spans:
        p = jnp.exp2((scores[:, at : at + n] - top) * np.float32(SCALE2))
        total = total + jnp.sum(p, axis=-1, keepdims=True)
        acc = acc + dot(p.astype(BF), kv[0:n, 128:])
    if last:
        rest[-2][0] = (acc / total).astype(BF)
    else:
        out, top_out, sum_out = rest[-4:-1]
        out[0] = acc
        top_out[0] = top
        sum_out[0] = total


def attention(q, kvs, before=None, last=False):
    rows = q.shape[1]
    keys = sum(kv.shape[0] // 128 * 128 for kv in kvs)

    def spec(r, c):
        return pl.BlockSpec((1, r, c), lambda i: (i, 0, 0))

    state = [spec(rows, c) for c in (HP, 1, 1)]
    shapes = [jax.ShapeDtypeStruct((4, rows, c), F32) for c in (HP, 1, 1)]
    return pl.pallas_call(
        functools.partial(attn_kernel, before is not None, last, len(kvs)),
        out_shape=jax.ShapeDtypeStruct((4, rows, HP), BF) if last else shapes,
        grid=(4,),
        in_specs=[spec(rows, HP)] + [whole(kv.shape) for kv in kvs] + (state if before else []),
        out_specs=spec(rows, HP) if last else state,
        scratch_shapes=[pltpu.VMEM((rows, keys), F32)],
        compiler_params=params(14),
        cost_estimate=cost(4 * 4 * rows * keys * HP, 5_000_000, 4 * rows * keys),
        name="attention",
    )(q, *kvs, *(before or ()))


def out_rows_kernel(pos, mine, theirs, w):
    y, g = pos[0], pos[1]
    for k in range(4):
        for back in range(4):
            at = pl.multiple_of(48 * (4 * lax.rem(y + 4 - back, 4) + (g ^ k)), 16)
            for c in range(4):
                top = 192 * (k // 2) + 48 * c
                w[pl.ds(at, 48), QW * c : QW * c + QW] = (mine, theirs)[k % 2][back, top : top + 48, :]


def out_rows(pos, mine, theirs):
    return pl.pallas_call(
        out_rows_kernel,
        out_shape=jax.ShapeDtypeStruct((HEADS * HD, D), BF),
        in_specs=[smem()] + [vmem()] * 2,
        out_specs=vmem(),
        compiler_params=params(8),
        cost_estimate=cost(0, 3_000_000),
        name="out_rows",
    )(pos, mine, theirs)


def out_kernel(pos, o0, o1, o2, o3, w, gain, k0, k1, k3, k2, lr, att_out, lr_out):
    y = pos[0]
    branch = None
    for m, o in enumerate((o0, o1, o2, o3)):
        at = pl.multiple_of(HD * lax.rem(y + m, 4), 16)
        part = dot(o[:, HP - HD :], w[pl.ds(at, HD), :])
        branch = part if m == 0 else branch + part
    scale = lax.rsqrt(jnp.mean(branch * branch, axis=-1, keepdims=True) + 1e-06)
    att = (branch * scale * gain[...]).astype(BF)
    att_out[...] = att
    rows = att.shape[0]
    r = lax.broadcasted_iota(jnp.int32, (rows // 16, rows), 0)
    c = lax.broadcasted_iota(jnp.int32, (rows // 16, rows), 1)
    pool = jnp.where(c // 16 == r, 1.0 / 16.0, 0.0).astype(BF)
    sides = None
    for m in range(4):
        at = pl.multiple_of(QW * lax.rem(y + 4 - m, 4), 128)
        row = (0, 3, 0, 1)[m] * rows
        tokens = (k0, k1, k2, k3)[m][row : row + rows, :]
        pooled = dot(pool, tokens) + dot(pool, att_out[:, pl.ds(at, QW)])
        part = dot(pooled.astype(BF), lr[pl.ds(at, QW), :])
        sides = part if m == 0 else sides + part
    lr_out[...] = sides.astype(BF)


def out_project(pos, os, w, gain, toks, lr):
    rows = os[0].shape[0]
    return pl.pallas_call(
        out_kernel,
        out_shape=(
            jax.ShapeDtypeStruct((rows, D), BF),
            jax.ShapeDtypeStruct((rows // 16, 256), BF),
        ),
        in_specs=[smem()] + [vmem()] * 11,
        out_specs=(vmem(), vmem()),
        compiler_params=params(12),
        cost_estimate=cost(2 * rows * HEADS * HD * D, 5_000_000, rows),
        name="out_project",
    )(pos, *os, w, gain, *toks, lr)


def pair_kernel(rows, cols, r0, r1, r2, r3, w, out, table, mixed):
    for d, r in enumerate((r0, r1, r2, r3)):
        table[8 * d : 8 * d + 8] = r[...].astype(F32).reshape(8, 8, 256)
    tiles = out.shape[0]
    for t in range(tiles):
        left = table[rows[t]][:, :128]
        right = table[cols[t]][:, 128:]
        z = gelu(left[:, None, :] + right[None, :, :])
        mixed[64 * t : 64 * t + 64, :] = z.reshape(64, 128).astype(BF)
    out[...] = dot(mixed[...], w[...]).reshape(tiles, 8, 8, 128).astype(BF)


def pair(rows, cols, sides, w):
    tiles = rows.shape[0]
    return pl.pallas_call(
        pair_kernel,
        out_shape=jax.ShapeDtypeStruct((tiles, 8, 8, 128), BF),
        in_specs=[smem()] * 2 + [vmem()] * 5,
        out_specs=vmem(),
        scratch_shapes=[pltpu.VMEM((32, 8, 256), F32), pltpu.VMEM((tiles * 64, 128), BF)],
        compiler_params=params(8),
        cost_estimate=cost(2 * tiles * 64 * 128 * 128, 1_000_000, tiles * 64 * 128),
        name="pair",
    )(rows, cols, *sides, w)


def shards(
    encoder_in,
    conv_weight,
    norm_gain,
    query_weight,
    key_weight,
    value_weight,
    out_weight,
    post_gain,
    left_weight,
    right_weight,
    pair_weight,
    tile_ids,
):
    seq = lax.axis_index("seq")
    y, j = seq // 4, seq % 4
    pos = jnp.stack([y, j]).astype(jnp.int32)

    msgs = messages(pos, conv_weight, encoder_in, query_weight, key_weight, value_weight)
    out_own = jnp.concatenate([out_weight[:, QW * c : QW * c + QW] for c in range(4)], axis=0)
    out_pair = xor_send(tie(out_own, msgs), 2)
    msgs = [msgs[0]] + [y_send(msgs[d], d) for d in (1, 2, 3)]
    pairs = encoder_in.reshape(BLOCK, 2 * CIN)
    msgs, pairs, out_pair = lax.optimization_barrier((msgs, pairs, out_pair))
    w_own, p_own = units(msgs)
    w_across = xor_send(w_own, 2)

    pairs = tie(pairs, w_own)
    rows_one, rows_three = y_send(pairs, 1), y_send(pairs, 3)
    low, high = halves(rows_one, rows_three, BLOCK // 2)
    rows_low, rows_high = y_send(low, 1), y_send(high, 3)
    w_units = [w_own, xor_send(w_own, 1), w_across, xor_send(w_across, 1)]
    p_own = tie(p_own, w_across)
    p_across = xor_send(p_own, 2)

    first, wall, edges = conv_call(
        conv_first_kernel, "conv_first", (3 * BLOCK, KW * CIN, 288), pos, pairs, rows_one, rows_three, *w_units
    )
    (tok_own,) = conv_call(
        conv_second_kernel, "conv_second", (4 * BLOCK,), pos, rows_low, rows_high, wall, edges, first
    )
    tok_own, p_across = lax.optimization_barrier((tok_own, p_across))
    tok_one, tok_three = y_send(tok_own, 1), y_send(tok_own, 3)
    p_units = [p_own, xor_send(p_own, 1), p_across, xor_send(p_across, 1)]
    tok_low, tok_high = halves(tok_one, tok_three, 2 * BLOCK)
    tok_low, tok_high = y_send(tok_low, 1), y_send(tok_high, 3)
    gain = norm_gain.reshape(4, 1, QW)
    q, kv = qkv(pos, [tok_own, tok_one, tok_three, tok_low, tok_high], gain, p_units)

    kv_across = xor_send(kv, 2)
    out_pair = tie(jnp.concatenate([out_own, out_pair]), kv)
    out_all = [out_pair] + [y_send(out_pair, d) for d in (1, 2, 3)]
    state = attention(q, [kv, xor_send(kv, 1)])
    kv_across, out_all = tie((kv_across, out_all), state)
    mixed = attention(q, [kv_across, xor_send(kv_across, 1)], state, True)
    os = [mixed[0]] + [y_send(mixed[d], 4 - d) for d in (1, 2, 3)]
    out_all = jnp.stack(tie(out_all, mixed))
    out_full = out_rows(pos, out_all, xor_send(out_all, 1))
    own_tokens = [tok_own, tok_one, tok_three, tok_high]

    lr = jnp.concatenate([left_weight, right_weight], axis=1)
    attended, sides = out_project(pos, os, out_full, post_gain.reshape(1, D), own_tokens, lr)

    row = jnp.stack([sides] + [xor_send(sides, k) for k in (1, 2, 3)])
    rows_all = [row] + [y_send(row, d) for d in (1, 2, 3)]

    row_table, col_table = np.triu_indices(32)
    matches = tile_ids[:, None] == jnp.arange(row_table.shape[0], dtype=jnp.int32)[None, :]

    def place(number):
        block = jnp.sum(jnp.where(matches, jnp.asarray(number, jnp.int32)[None, :], 0), axis=1)
        owner = block // 2
        back = jnp.mod(y - owner // 4, 4)
        rel = jnp.bitwise_xor(j, owner % 4)
        return (back * 4 + rel) * 2 + block % 2

    pair_tiles = pair(place(row_table), place(col_table), rows_all, pair_weight)
    return (attended, pair_tiles)


def solution(mesh):
    in_specs = (
        P(("dp", "seq"), None),
        P(None, "seq", None),
        P(),
        P("seq", None),
        P("seq", None),
        P("seq", None),
        P("seq", None),
        P(),
        P(),
        P(),
        P(),
        P(("dp", "seq")),
    )
    out_specs = (P(("dp", "seq"), None), P(("dp", "seq"), None, None, None))
    return jax.shard_map(shards, mesh=mesh, in_specs=in_specs, out_specs=out_specs, check_vma=False)
```

```python
import functools

import jax
import jax.numpy as jnp
import numpy as np
from jax import lax
from jax.experimental import pallas as pl
from jax.experimental.pallas import tpu as pltpu
from jax.sharding import PartitionSpec as P

HEADS = 4
BLOCK = 256
HD = 192
HP = 256
D = 1536
QW = 384
CIN = 768
KW = 5
BF = jnp.bfloat16
F32 = jnp.float32
SCALE2 = float(HD ** (-0.5) * np.log2(np.e))


def params(mib):
    return pltpu.CompilerParams(vmem_limit_bytes=mib * 1024 * 1024)


def cost(flops, nbytes, trans=0):
    return pl.CostEstimate(flops=flops, bytes_accessed=nbytes, transcendentals=trans)


def xor_send(x, m):
    return lax.ppermute(x, "seq", [(s, s ^ m) for s in range(16)])


def y_send(x, d):
    return lax.ppermute(x, "seq", [(s, (s + 4 * d) % 16) for s in range(16)])


def tie(x, *others):
    return lax.optimization_barrier((x,) + others)[0]


def gelu(x):
    return 0.5 * x * (1.0 + lax.erf(x * np.float32(np.sqrt(0.5))))


def whole(shape):
    zeros = (0,) * len(shape)
    return pl.BlockSpec(shape, lambda *_: zeros)


def dot(a, b):
    return jnp.dot(a, b, preferred_element_type=F32)


def vmem():
    return pl.BlockSpec(memory_space=pltpu.VMEM)


def smem():
    return pl.BlockSpec(memory_space=pltpu.SMEM)


MSG_EDGE, MSG_KV, MSG_Q, MSG = 240, 256, 352, 400
W_EDGE, W_ALL = 960, 1024
HEAD_ROWS = MSG - MSG_KV


def message_kernel(pos, w, rows, wq, wk, wv, o0, o1, o2, o3, w_in, ends, q_in, k_in, v_in, sems):
    copies = [pltpu.make_async_copy(w.at[t], w_in.at[t], sems.at[t]) for t in range(KW)]
    last = rows.shape[0] - 16
    copies.append(pltpu.make_async_copy(rows.at[pl.ds(0, 16)], ends.at[0], sems.at[KW]))
    copies.append(pltpu.make_async_copy(rows.at[pl.ds(last, 16)], ends.at[1], sems.at[KW + 1]))
    for n, (src, dst) in enumerate(((wq, q_in), (wk, k_in), (wv, v_in))):
        copies.append(pltpu.make_async_copy(src, dst, sems.at[KW + 2 + n]))
    for copy in copies:
        copy.start()
    for copy in copies:
        copy.wait()
    at = lax.broadcasted_iota(jnp.int32, (16, QW), 0)
    edges = jnp.zeros((16, QW), F32)
    first, final = ends[0].astype(F32), ends[1].astype(F32)
    lines = [first[0:1], first[1:2], final[14:15], final[15:16]]
    for n in range(8):
        edges = jnp.where(at == n, lines[n // 2][:, (n % 2) * QW : (n % 2) * QW + QW], edges)
    edges = edges.astype(BF)
    outs = (o0, o1, o2, o3)
    for d, out in enumerate(outs):
        cols = pl.ds(pl.multiple_of(QW * lax.rem(pos[0] + d, 4), 128), QW)
        for t in range(KW):
            out[48 * t : 48 * t + 48, :] = w_in[t, :, cols]
        out[MSG_EDGE:MSG_KV, :] = edges
    for place in range(4):

        @pl.when(pos[0] == place)
        def _():
            for d, out in enumerate(outs):
                head = (place + d) % 4
                cols = slice(HD * head, HD * head + HD)
                out[MSG_KV:MSG_Q, :] = jnp.concatenate([k_in[:, cols], v_in[:, cols]], axis=1)
                out[MSG_Q:MSG, :] = jnp.concatenate([q_in[0:48, cols], q_in[48:96, cols]], axis=1)


def hbm():
    return pl.BlockSpec(memory_space=pltpu.HBM)


def messages(pos, w, rows, wq, wk, wv):
    return pl.pallas_call(
        message_kernel,
        out_shape=[jax.ShapeDtypeStruct((MSG, QW), BF)] * 4,
        in_specs=[smem()] + [hbm()] * 5,
        out_specs=[vmem()] * 4,
        scratch_shapes=[pltpu.VMEM((KW, 48, D), BF), pltpu.VMEM((2, 16, CIN), BF)]
        + [pltpu.VMEM((96, HEADS * HD), BF)] * 3
        + [pltpu.SemaphoreType.DMA((KW + 5,))],
        compiler_params=params(56),
        cost_estimate=cost(0, 3_000_000),
        name="messages",
    )(pos, w, rows, wq, wk, wv)


def unit_kernel(m0, m1, m2, m3, w_out, p_out):
    for d, m in enumerate((m0, m1, m2, m3)):
        w_out[MSG_EDGE * d : MSG_EDGE * d + MSG_EDGE, :] = m[0:MSG_EDGE, :]
        w_out[W_EDGE + 16 * d : W_EDGE + 16 * d + 16, :] = m[MSG_EDGE:MSG_KV, :]
        p_out[HEAD_ROWS * d : HEAD_ROWS * d + HEAD_ROWS, :] = m[MSG_KV:MSG, :]


def units(msgs):
    return pl.pallas_call(
        unit_kernel,
        out_shape=[jax.ShapeDtypeStruct((r, QW), BF) for r in (W_ALL, 4 * HEAD_ROWS)],
        in_specs=[vmem()] * 4,
        out_specs=[vmem()] * 2,
        compiler_params=params(8),
        cost_estimate=cost(0, 1_500_000),
        name="units",
    )(*msgs)


def halves_kernel(one, three, low, high):
    cut = low.shape[0]
    low[...] = one[0:cut, :]
    high[...] = three[cut : 2 * cut, :]


def halves(one, three, cut):
    return pl.pallas_call(
        halves_kernel,
        out_shape=[jax.ShapeDtypeStruct((cut, one.shape[1]), BF)] * 2,
        in_specs=[vmem()] * 2,
        out_specs=[vmem()] * 2,
        compiler_params=params(8),
        cost_estimate=cost(0, 1_000_000),
        name="halves",
    )(one, three)


def place_weights(pos, unit_refs, wall, edges):
    y, g = pos[0], pos[1]
    edges[0:16, :] = jnp.zeros((16, QW), BF)
    edges[272:288, :] = jnp.zeros((16, QW), BF)
    for k, unit in enumerate(unit_refs):
        for back in range(4):
            device = 4 * lax.rem(y + 4 - back, 4) + (g ^ k)
            at = pl.multiple_of(48 * device, 16)
            for t in range(KW):
                start = MSG_EDGE * back + 48 * t
                wall[pl.ds(at + CIN * t, 48), :] = unit[start : start + 48, :]
            lines = W_EDGE + 16 * back
            edges[pl.ds(pl.multiple_of(16 * (device + 1), 16), 16), :] = unit[lines : lines + 16, :]


def block_tokens(device, block, wall, edges):
    at = lax.broadcasted_iota(jnp.int32, (16, 2 * CIN), 0)

    def beside(place, line, row):
        rows = edges[pl.ds(pl.multiple_of(16 * place, 16), 16), :].astype(F32)
        joined = jnp.concatenate([rows[line + n : line + n + 1] for n in range(4)], axis=1)
        return jnp.where(at == row, joined, 0.0).astype(BF)

    near = jnp.concatenate([beside(device, 4, 15), block, beside(device + 2, 0, 0)], axis=0)
    pm, p0, pp = (near[15 + n : 15 + n + BLOCK] for n in range(3))
    halves_of = [v[:, n : n + CIN] for v in (pm, p0, pp) for n in (0, CIN)]
    acc = None
    for t in range(KW):
        pair = jnp.concatenate(halves_of[t : t + 2], axis=0)
        part = dot(pair, wall[CIN * t : CIN * t + CIN, :])
        acc = part if t == 0 else acc + part
    return jnp.maximum(gelu(acc[:BLOCK]), gelu(acc[BLOCK:])).astype(BF)


def device_at(pos, back):
    return 4 * lax.rem(pos[0] + 4 - back, 4) + pos[1]


def conv_first_kernel(pos, b0, b1, b3, u0, u1, u2, u3, out, wall, edges):
    place_weights(pos, (u0, u1, u2, u3), wall, edges)
    for n, (back, block) in enumerate(((0, b0), (1, b1), (3, b3))):
        out[BLOCK * n : BLOCK * n + BLOCK, :] = block_tokens(device_at(pos, back), block[...], wall, edges)


def conv_second_kernel(pos, low, high, wall, edges, first, out):
    block = jnp.concatenate([low[...], high[...]], axis=0)
    out[0 : 2 * BLOCK, :] = first[0 : 2 * BLOCK, :]
    out[2 * BLOCK : 3 * BLOCK, :] = block_tokens(device_at(pos, 2), block, wall, edges)
    out[3 * BLOCK :, :] = first[2 * BLOCK :, :]


def conv_call(kernel, name, shapes, *operands):
    return pl.pallas_call(
        kernel,
        out_shape=[jax.ShapeDtypeStruct((r, QW), BF) for r in shapes],
        in_specs=[smem()] + [vmem()] * (len(operands) - 1),
        out_specs=[vmem()] * len(shapes),
        compiler_params=params(14),
        cost_estimate=cost(2 * 2 * BLOCK * KW * CIN * QW, 8_000_000, 4 * BLOCK * QW),
        name=name,
    )(*operands)


def qkv_kernel(pos, t0, t1, t3, low, high, gain, u0, u1, u2, u3, q_out, kv_out, wall):
    y, g = pos[0], pos[1]
    gap = jnp.zeros((48, HP - HD), BF)
    for k, unit in enumerate((u0, u1, u2, u3)):
        for back in range(4):
            at = pl.multiple_of(96 * (4 * lax.rem(y + 4 - back, 4) + (g ^ k)), 16)
            top = HEAD_ROWS * back
            wall[pl.ds(at, 96), HP:] = unit[top : top + 96, :]
            for side in range(2):
                rows = unit[top + 96 : top + 144, HD * side : HD * side + HD]
                wall[pl.ds(at + 48 * side, 48), 0:HP] = jnp.concatenate([rows, gap], axis=1)

    def tokens(back, block):
        at = (block - back) % 4
        ref = {0: t0, 1: t1, 2: (low, high)[at // 2], 3: t3}[back]
        at = at % 2 if back == 2 else at
        return ref[BLOCK * at : BLOCK * at + BLOCK, :].astype(F32)

    for block in range(4):
        squares = 0.0
        for back in range(4):
            vals = tokens(back, block)
            squares = squares + jnp.sum(vals * vals, axis=-1, keepdims=True)
        scale = lax.rsqrt(squares * np.float32(1.0 / D) + 1e-06)
        acc = 0.0
        for back in range(4):
            place = lax.rem(y + 4 - back, 4)
            normed = (tokens(back, block) * scale * gain[place]).astype(BF)
            acc = acc + dot(normed, wall[pl.ds(pl.multiple_of(QW * place, 128), QW), :])
        done = acc.astype(BF)
        q_out[block] = done[:, :HP]
        kv_out[BLOCK * block : BLOCK * block + BLOCK, :] = done[:, HP:]


def qkv(pos, tokens, gain, head_units):
    rows = tokens[0].shape[0]
    return pl.pallas_call(
        qkv_kernel,
        out_shape=[jax.ShapeDtypeStruct((4, BLOCK, HP), BF), jax.ShapeDtypeStruct((rows, QW), BF)],
        in_specs=[smem()] + [vmem()] * 10,
        out_specs=[vmem()] * 2,
        scratch_shapes=[pltpu.VMEM((D, HP + QW), BF)],
        compiler_params=params(14),
        cost_estimate=cost(2 * rows * D * 640, 6_000_000, rows),
        name="qkv",
    )(pos, *tokens, gain, *head_units)


def attn_kernel(merge, last, n_kv, *refs):
    queries, kvs, rest = refs[0], refs[1 : 1 + n_kv], refs[1 + n_kv :]
    scores = rest[-1]
    for block in range(4):
        q, slot = queries[block], block % 2
        top, at = None, 0
        spans = []
        for kv in kvs:
            n = kv.shape[0]
            s = lax.dot_general(q, kv[:, :HP], (((1,), (1,)), ((), ())), preferred_element_type=F32)
            scores[slot, :, at : at + n] = s
            most = jnp.max(s, axis=-1, keepdims=True)
            top = most if top is None else jnp.maximum(top, most)
            spans.append((kv, at, n))
            at += n
        if merge:
            acc_in, top_in, sum_in = rest[:3]
            top = jnp.maximum(top, top_in[block])
            fade = jnp.exp2((top_in[block] - top) * np.float32(SCALE2))
            total, acc = sum_in[block] * fade, acc_in[block] * fade
        else:
            total, acc = 0.0, 0.0
        for kv, at, n in spans:
            p = jnp.exp2((scores[slot, :, at : at + n] - top) * np.float32(SCALE2))
            total = total + jnp.sum(p, axis=-1, keepdims=True)
            acc = acc + dot(p.astype(BF), kv[:, 128:])
        if last:
            done = (acc / total).astype(BF)[:, HP - HD :]
            half = done.shape[0] // 2
            rest[block - 5][...] = jnp.concatenate([done[:half], done[half:]], axis=1)
        else:
            out, top_out, sum_out = rest[-4:-1]
            out[block] = acc
            top_out[block] = top
            sum_out[block] = total


def attention(q, kvs, before=None, last=False):
    rows = q.shape[1]
    keys = sum(kv.shape[0] for kv in kvs)
    state = [jax.ShapeDtypeStruct((4, rows, c), F32) for c in (HP, 1, 1)]
    result = [jax.ShapeDtypeStruct((rows // 2, QW), BF)] * 4
    operands = (q, *kvs, *(before or ()))
    return pl.pallas_call(
        functools.partial(attn_kernel, before is not None, last, len(kvs)),
        out_shape=result if last else state,
        in_specs=[vmem()] * len(operands),
        out_specs=[vmem()] * (4 if last else 3),
        scratch_shapes=[pltpu.VMEM((2, rows, keys), F32)],
        compiler_params=params(16),
        cost_estimate=cost(4 * 4 * rows * keys * HP, 5_000_000, 4 * rows * keys),
        name="attention",
    )(*operands)


def out_rows_kernel(pos, mine, theirs, w):
    y, g = pos[0], pos[1]
    for k in range(4):
        for back in range(4):
            at = pl.multiple_of(48 * (4 * lax.rem(y + 4 - back, 4) + (g ^ k)), 16)
            for c in range(4):
                top = 192 * (k // 2) + 48 * c
                w[pl.ds(at, 48), QW * c : QW * c + QW] = (mine, theirs)[k % 2][back, top : top + 48, :]


def out_rows(pos, mine, theirs):
    return pl.pallas_call(
        out_rows_kernel,
        out_shape=jax.ShapeDtypeStruct((HEADS * HD, D), BF),
        in_specs=[smem()] + [vmem()] * 2,
        out_specs=vmem(),
        compiler_params=params(8),
        cost_estimate=cost(0, 3_000_000),
        name="out_rows",
    )(pos, mine, theirs)


def out_kernel(pos, o0, o1, o2, o3, w, gain, k0, k1, k3, k2, lr, att_out, lr_out):
    y = pos[0]
    branch = None
    for m, o in enumerate((o0, o1, o2, o3)):
        at = pl.multiple_of(HD * lax.rem(y + m, 4), 16)
        heads = jnp.concatenate([o[:, :HD], o[:, HD:]], axis=0)
        part = dot(heads, w[pl.ds(at, HD), :])
        branch = part if m == 0 else branch + part
    scale = lax.rsqrt(jnp.mean(branch * branch, axis=-1, keepdims=True) + 1e-06)
    att = (branch * scale * gain[...]).astype(BF)
    att_out[...] = att
    rows = att.shape[0]
    r = lax.broadcasted_iota(jnp.int32, (rows // 16, rows), 0)
    c = lax.broadcasted_iota(jnp.int32, (rows // 16, rows), 1)
    pool = jnp.where(c // 16 == r, 1.0 / 16.0, 0.0).astype(BF)
    sides = None
    for m in range(4):
        at = pl.multiple_of(QW * lax.rem(y + 4 - m, 4), 128)
        row = (0, 3, 0, 1)[m] * rows
        tokens = (k0, k1, k2, k3)[m][row : row + rows, :]
        pooled = dot(pool, tokens) + dot(pool, att_out[:, pl.ds(at, QW)])
        part = dot(pooled.astype(BF), lr[pl.ds(at, QW), :])
        sides = part if m == 0 else sides + part
    lr_out[...] = sides.astype(BF)


def out_project(pos, os, w, gain, toks, lr):
    rows = 2 * os[0].shape[0]
    return pl.pallas_call(
        out_kernel,
        out_shape=(
            jax.ShapeDtypeStruct((rows, D), BF),
            jax.ShapeDtypeStruct((rows // 16, 256), BF),
        ),
        in_specs=[smem()] + [vmem()] * 11,
        out_specs=(vmem(), vmem()),
        compiler_params=params(12),
        cost_estimate=cost(2 * rows * HEADS * HD * D, 5_000_000, rows),
        name="out_project",
    )(pos, *os, w, gain, *toks, lr)


def pair_kernel(rows, cols, r0, r1, r2, r3, w, out, table, mixed):
    for d, r in enumerate((r0, r1, r2, r3)):
        table[8 * d : 8 * d + 8] = r[...].astype(F32).reshape(8, 8, 256)
    tiles = out.shape[0]
    for t in range(tiles):
        left = table[rows[t]][:, :128]
        right = table[cols[t]][:, 128:]
        z = gelu(left[:, None, :] + right[None, :, :])
        mixed[64 * t : 64 * t + 64, :] = z.reshape(64, 128).astype(BF)
    out[...] = dot(mixed[...], w[...]).reshape(tiles, 8, 8, 128).astype(BF)


def pair(rows, cols, sides, w):
    tiles = rows.shape[0]
    return pl.pallas_call(
        pair_kernel,
        out_shape=jax.ShapeDtypeStruct((tiles, 8, 8, 128), BF),
        in_specs=[smem()] * 2 + [vmem()] * 5,
        out_specs=vmem(),
        scratch_shapes=[pltpu.VMEM((32, 8, 256), F32), pltpu.VMEM((tiles * 64, 128), BF)],
        compiler_params=params(8),
        cost_estimate=cost(2 * tiles * 64 * 128 * 128, 1_000_000, tiles * 64 * 128),
        name="pair",
    )(rows, cols, *sides, w)


def shards(
    encoder_in,
    conv_weight,
    norm_gain,
    query_weight,
    key_weight,
    value_weight,
    out_weight,
    post_gain,
    left_weight,
    right_weight,
    pair_weight,
    tile_ids,
):
    seq = lax.axis_index("seq")
    y, j = seq // 4, seq % 4
    pos = jnp.stack([y, j]).astype(jnp.int32)

    msgs = messages(pos, conv_weight, encoder_in, query_weight, key_weight, value_weight)
    out_own = jnp.concatenate([out_weight[:, QW * c : QW * c + QW] for c in range(4)], axis=0)
    out_pair = xor_send(tie(out_own, msgs), 2)
    msgs = [msgs[0]] + [y_send(msgs[d], d) for d in (1, 2, 3)]
    pairs = encoder_in.reshape(BLOCK, 2 * CIN)
    msgs, pairs, out_pair = lax.optimization_barrier((msgs, pairs, out_pair))
    w_own, p_own = units(msgs)
    w_across = xor_send(w_own, 2)

    rows_one, rows_three = y_send(pairs, 1), y_send(pairs, 3)
    low, high = halves(rows_one, rows_three, BLOCK // 2)
    rows_low, rows_high = y_send(low, 1), y_send(high, 3)
    w_units = [w_own, xor_send(w_own, 1), w_across, xor_send(w_across, 1)]
    p_own = tie(p_own, w_across)
    p_across = xor_send(p_own, 2)

    first, wall, edges = conv_call(
        conv_first_kernel, "conv_first", (3 * BLOCK, KW * CIN, 288), pos, pairs, rows_one, rows_three, *w_units
    )
    (tok_own,) = conv_call(
        conv_second_kernel, "conv_second", (4 * BLOCK,), pos, rows_low, rows_high, wall, edges, first
    )
    tok_own, p_across = lax.optimization_barrier((tok_own, p_across))
    tok_one, tok_three = y_send(tok_own, 1), y_send(tok_own, 3)
    p_units = [p_own, xor_send(p_own, 1), p_across, xor_send(p_across, 1)]
    tok_low, tok_high = halves(tok_one, tok_three, 2 * BLOCK)
    tok_low, tok_high = y_send(tok_low, 1), y_send(tok_high, 3)
    gain = norm_gain.reshape(4, 1, QW)
    q, kv = qkv(pos, [tok_own, tok_one, tok_three, tok_low, tok_high], gain, p_units)

    kv_across = xor_send(kv, 2)
    out_pair = tie(jnp.concatenate([out_own, out_pair]), kv)
    out_all = [out_pair] + [y_send(out_pair, d) for d in (1, 2, 3)]
    state = attention(q, [kv, xor_send(kv, 1)])
    kv_across, out_all = tie((kv_across, out_all), state)
    kv_diagonal = xor_send(kv_across, 1)
    state = attention(q, [kv_across], state)
    mixed = attention(q, [kv_diagonal], state, True)
    os = [mixed[0]] + [y_send(mixed[d], 4 - d) for d in (1, 2, 3)]
    out_all = jnp.stack(tie(out_all, mixed))
    out_full = out_rows(pos, out_all, xor_send(out_all, 1))
    own_tokens = [tok_own, tok_one, tok_three, tok_high]

    lr = jnp.concatenate([left_weight, right_weight], axis=1)
    attended, sides = out_project(pos, os, out_full, post_gain.reshape(1, D), own_tokens, lr)

    row = jnp.stack([sides] + [xor_send(sides, k) for k in (1, 2, 3)])
    rows_all = [row] + [y_send(row, d) for d in (1, 2, 3)]

    row_table, col_table = np.triu_indices(32)
    matches = tile_ids[:, None] == jnp.arange(row_table.shape[0], dtype=jnp.int32)[None, :]

    def place(number):
        block = jnp.sum(jnp.where(matches, jnp.asarray(number, jnp.int32)[None, :], 0), axis=1)
        owner = block // 2
        back = jnp.mod(y - owner // 4, 4)
        rel = jnp.bitwise_xor(j, owner % 4)
        return (back * 4 + rel) * 2 + block % 2

    pair_tiles = pair(place(row_table), place(col_table), rows_all, pair_weight)
    return (attended, pair_tiles)


def solution(mesh):
    in_specs = (
        P(("dp", "seq"), None),
        P(None, "seq", None),
        P(),
        P("seq", None),
        P("seq", None),
        P("seq", None),
        P("seq", None),
        P(),
        P(),
        P(),
        P(),
        P(("dp", "seq")),
    )
    out_specs = (P(("dp", "seq"), None), P(("dp", "seq"), None, None, None))
    return jax.shard_map(shards, mesh=mesh, in_specs=in_specs, out_specs=out_specs, check_vma=False)
```

```python
import functools

import jax
import jax.numpy as jnp
import numpy as np
from jax import lax
from jax.experimental import pallas as pl
from jax.experimental.pallas import tpu as pltpu
from jax.sharding import PartitionSpec as P

HEADS = 4
BLOCK = 256
HD = 192
HP = 256
D = 1536
QW = 384
CIN = 768
KW = 5
BF = jnp.bfloat16
F32 = jnp.float32
SCALE2 = float(HD ** (-0.5) * np.log2(np.e))


def params(mib):
    return pltpu.CompilerParams(vmem_limit_bytes=mib * 1024 * 1024)


def cost(flops, nbytes, trans=0):
    return pl.CostEstimate(flops=flops, bytes_accessed=nbytes, transcendentals=trans)


def xor_send(x, m):
    return lax.ppermute(x, "seq", [(s, s ^ m) for s in range(16)])


def y_send(x, d):
    return lax.ppermute(x, "seq", [(s, (s + 4 * d) % 16) for s in range(16)])


def tie(x, *others):
    return lax.optimization_barrier((x,) + others)[0]


def gelu(x):
    return 0.5 * x * (1.0 + lax.erf(x * np.float32(np.sqrt(0.5))))


def whole(shape):
    zeros = (0,) * len(shape)
    return pl.BlockSpec(shape, lambda *_: zeros)


def dot(a, b):
    return jnp.dot(a, b, preferred_element_type=F32)


def vmem():
    return pl.BlockSpec(memory_space=pltpu.VMEM)


def smem():
    return pl.BlockSpec(memory_space=pltpu.SMEM)


MSG_EDGE, MSG_KV, MSG_Q, MSG = 240, 256, 352, 400
W_EDGE, W_ALL = 960, 1024
HEAD_ROWS = MSG - MSG_KV


def message_kernel(pos, w, rows, wq, wk, wv, o0, o1, o2, o3, w_in, ends, q_in, k_in, v_in, sems):
    copies = [pltpu.make_async_copy(w.at[t], w_in.at[t], sems.at[t]) for t in range(KW)]
    last = rows.shape[0] - 16
    copies.append(pltpu.make_async_copy(rows.at[pl.ds(0, 16)], ends.at[0], sems.at[KW]))
    copies.append(pltpu.make_async_copy(rows.at[pl.ds(last, 16)], ends.at[1], sems.at[KW + 1]))
    for n, (src, dst) in enumerate(((wq, q_in), (wk, k_in), (wv, v_in))):
        copies.append(pltpu.make_async_copy(src, dst, sems.at[KW + 2 + n]))
    for copy in copies:
        copy.start()
    for copy in copies:
        copy.wait()
    at = lax.broadcasted_iota(jnp.int32, (16, QW), 0)
    edges = jnp.zeros((16, QW), F32)
    first, final = ends[0].astype(F32), ends[1].astype(F32)
    lines = [first[0:1], first[1:2], final[14:15], final[15:16]]
    for n in range(8):
        edges = jnp.where(at == n, lines[n // 2][:, (n % 2) * QW : (n % 2) * QW + QW], edges)
    edges = edges.astype(BF)
    outs = (o0, o1, o2, o3)
    for d, out in enumerate(outs):
        cols = pl.ds(pl.multiple_of(QW * lax.rem(pos[0] + d, 4), 128), QW)
        for t in range(KW):
            out[48 * t : 48 * t + 48, :] = w_in[t, :, cols]
        out[MSG_EDGE:MSG_KV, :] = edges
    for place in range(4):

        @pl.when(pos[0] == place)
        def _():
            for d, out in enumerate(outs):
                head = (place + d) % 4
                cols = slice(HD * head, HD * head + HD)
                out[MSG_KV:MSG_Q, :] = jnp.concatenate([k_in[:, cols], v_in[:, cols]], axis=1)
                out[MSG_Q:MSG, :] = jnp.concatenate([q_in[0:48, cols], q_in[48:96, cols]], axis=1)


def hbm():
    return pl.BlockSpec(memory_space=pltpu.HBM)


def messages(pos, w, rows, wq, wk, wv):
    return pl.pallas_call(
        message_kernel,
        out_shape=[jax.ShapeDtypeStruct((MSG, QW), BF)] * 4,
        in_specs=[smem()] + [hbm()] * 5,
        out_specs=[vmem()] * 4,
        scratch_shapes=[pltpu.VMEM((KW, 48, D), BF), pltpu.VMEM((2, 16, CIN), BF)]
        + [pltpu.VMEM((96, HEADS * HD), BF)] * 3
        + [pltpu.SemaphoreType.DMA((KW + 5,))],
        compiler_params=params(56),
        cost_estimate=cost(0, 3_000_000),
        name="messages",
    )(pos, w, rows, wq, wk, wv)


def unit_kernel(m0, m1, m2, m3, w_out, p_out):
    for d, m in enumerate((m0, m1, m2, m3)):
        w_out[MSG_EDGE * d : MSG_EDGE * d + MSG_EDGE, :] = m[0:MSG_EDGE, :]
        w_out[W_EDGE + 16 * d : W_EDGE + 16 * d + 16, :] = m[MSG_EDGE:MSG_KV, :]
        p_out[HEAD_ROWS * d : HEAD_ROWS * d + HEAD_ROWS, :] = m[MSG_KV:MSG, :]


def units(msgs):
    return pl.pallas_call(
        unit_kernel,
        out_shape=[jax.ShapeDtypeStruct((r, QW), BF) for r in (W_ALL, 4 * HEAD_ROWS)],
        in_specs=[vmem()] * 4,
        out_specs=[vmem()] * 2,
        compiler_params=params(8),
        cost_estimate=cost(0, 1_500_000),
        name="units",
    )(*msgs)


def halves_kernel(one, three, low, high):
    cut = low.shape[0]
    low[...] = one[0:cut, :]
    high[...] = three[cut : 2 * cut, :]


def halves(one, three, cut):
    return pl.pallas_call(
        halves_kernel,
        out_shape=[jax.ShapeDtypeStruct((cut, one.shape[1]), BF)] * 2,
        in_specs=[vmem()] * 2,
        out_specs=[vmem()] * 2,
        compiler_params=params(8),
        cost_estimate=cost(0, 1_000_000),
        name="halves",
    )(one, three)


def place_weights(pos, unit_refs, wall, edges):
    y, g = pos[0], pos[1]
    edges[0:16, :] = jnp.zeros((16, QW), BF)
    edges[272:288, :] = jnp.zeros((16, QW), BF)
    for k, unit in enumerate(unit_refs):
        for back in range(4):
            device = 4 * lax.rem(y + 4 - back, 4) + (g ^ k)
            at = pl.multiple_of(48 * device, 16)
            for t in range(KW):
                start = MSG_EDGE * back + 48 * t
                wall[pl.ds(at + CIN * t, 48), :] = unit[start : start + 48, :]
            lines = W_EDGE + 16 * back
            edges[pl.ds(pl.multiple_of(16 * (device + 1), 16), 16), :] = unit[lines : lines + 16, :]


def block_tokens(device, block, wall, edges):
    at = lax.broadcasted_iota(jnp.int32, (16, 2 * CIN), 0)

    def beside(place, line, row):
        rows = edges[pl.ds(pl.multiple_of(16 * place, 16), 16), :].astype(F32)
        joined = jnp.concatenate([rows[line + n : line + n + 1] for n in range(4)], axis=1)
        return jnp.where(at == row, joined, 0.0).astype(BF)

    near = jnp.concatenate([beside(device, 4, 15), block, beside(device + 2, 0, 0)], axis=0)
    pm, p0, pp = (near[15 + n : 15 + n + BLOCK] for n in range(3))
    halves_of = [v[:, n : n + CIN] for v in (pm, p0, pp) for n in (0, CIN)]
    acc = None
    for t in range(KW):
        pair = jnp.concatenate(halves_of[t : t + 2], axis=0)
        part = dot(pair, wall[CIN * t : CIN * t + CIN, :])
        acc = part if t == 0 else acc + part
    return jnp.maximum(gelu(acc[:BLOCK]), gelu(acc[BLOCK:])).astype(BF)


def device_at(pos, back):
    return 4 * lax.rem(pos[0] + 4 - back, 4) + pos[1]


def conv_first_kernel(pos, b0, b1, b3, u0, u1, u2, u3, out, wall, edges):
    place_weights(pos, (u0, u1, u2, u3), wall, edges)
    for n, (back, block) in enumerate(((0, b0), (1, b1), (3, b3))):
        out[BLOCK * n : BLOCK * n + BLOCK, :] = block_tokens(device_at(pos, back), block[...], wall, edges)


def conv_second_kernel(pos, low, high, wall, edges, first, out):
    block = jnp.concatenate([low[...], high[...]], axis=0)
    out[0 : 2 * BLOCK, :] = first[0 : 2 * BLOCK, :]
    out[2 * BLOCK : 3 * BLOCK, :] = block_tokens(device_at(pos, 2), block, wall, edges)
    out[3 * BLOCK :, :] = first[2 * BLOCK :, :]


def conv_call(kernel, name, shapes, *operands):
    return pl.pallas_call(
        kernel,
        out_shape=[jax.ShapeDtypeStruct((r, QW), BF) for r in shapes],
        in_specs=[smem()] + [vmem()] * (len(operands) - 1),
        out_specs=[vmem()] * len(shapes),
        compiler_params=params(14),
        cost_estimate=cost(2 * 2 * BLOCK * KW * CIN * QW, 8_000_000, 4 * BLOCK * QW),
        name=name,
    )(*operands)


def qkv_kernel(pos, t0, t1, t3, low, high, gain, u0, u1, u2, u3, q_out, kv_out, wall):
    y, g = pos[0], pos[1]
    gap = jnp.zeros((48, HP - HD), BF)
    for k, unit in enumerate((u0, u1, u2, u3)):
        for back in range(4):
            at = pl.multiple_of(96 * (4 * lax.rem(y + 4 - back, 4) + (g ^ k)), 16)
            top = HEAD_ROWS * back
            wall[pl.ds(at, 96), HP:] = unit[top : top + 96, :]
            for side in range(2):
                rows = unit[top + 96 : top + 144, HD * side : HD * side + HD]
                wall[pl.ds(at + 48 * side, 48), 0:HP] = jnp.concatenate([rows, gap], axis=1)

    def tokens(back, block):
        at = (block - back) % 4
        ref = {0: t0, 1: t1, 2: (low, high)[at // 2], 3: t3}[back]
        at = at % 2 if back == 2 else at
        return ref[BLOCK * at : BLOCK * at + BLOCK, :].astype(F32)

    for block in range(4):
        squares = 0.0
        for back in range(4):
            vals = tokens(back, block)
            squares = squares + jnp.sum(vals * vals, axis=-1, keepdims=True)
        scale = lax.rsqrt(squares * np.float32(1.0 / D) + 1e-06)
        acc = 0.0
        for back in range(4):
            place = lax.rem(y + 4 - back, 4)
            normed = (tokens(back, block) * scale * gain[place]).astype(BF)
            acc = acc + dot(normed, wall[pl.ds(pl.multiple_of(QW * place, 128), QW), :])
        done = acc.astype(BF)
        q_out[block] = done[:, :HP]
        kv_out[BLOCK * block : BLOCK * block + BLOCK, :] = done[:, HP:]


def qkv(pos, tokens, gain, head_units):
    rows = tokens[0].shape[0]
    return pl.pallas_call(
        qkv_kernel,
        out_shape=[jax.ShapeDtypeStruct((4, BLOCK, HP), BF), jax.ShapeDtypeStruct((rows, QW), BF)],
        in_specs=[smem()] + [vmem()] * 10,
        out_specs=[vmem()] * 2,
        scratch_shapes=[pltpu.VMEM((D, HP + QW), BF)],
        compiler_params=params(14),
        cost_estimate=cost(2 * rows * D * 640, 6_000_000, rows),
        name="qkv",
    )(pos, *tokens, gain, *head_units)


def attn_kernel(merge, last, n_kv, *refs):
    queries, kvs, rest = refs[0], refs[1 : 1 + n_kv], refs[1 + n_kv :]
    scores = rest[-1]
    for block in range(4):
        q, slot = queries[block], block % 2
        top, at = None, 0
        spans = []
        for kv in kvs:
            n = kv.shape[0]
            s = lax.dot_general(q, kv[:, :HP], (((1,), (1,)), ((), ())), preferred_element_type=F32)
            scores[slot, :, at : at + n] = s
            most = jnp.max(s, axis=-1, keepdims=True)
            top = most if top is None else jnp.maximum(top, most)
            spans.append((kv, at, n))
            at += n
        if merge:
            acc_in, top_in, sum_in = rest[:3]
            top = jnp.maximum(top, top_in[block])
            fade = jnp.exp2((top_in[block] - top) * np.float32(SCALE2))
            total, acc = sum_in[block] * fade, acc_in[block] * fade
        else:
            total, acc = 0.0, 0.0
        for kv, at, n in spans:
            p = jnp.exp2((scores[slot, :, at : at + n] - top) * np.float32(SCALE2))
            total = total + jnp.sum(p, axis=-1, keepdims=True)
            acc = acc + dot(p.astype(BF), kv[:, 128:])
        if last:
            done = (acc / total).astype(BF)[:, HP - HD :]
            half = done.shape[0] // 2
            rest[block - 5][...] = jnp.concatenate([done[:half], done[half:]], axis=1)
        else:
            out, top_out, sum_out = rest[-4:-1]
            out[block] = acc
            top_out[block] = top
            sum_out[block] = total


def attention(q, kvs, before=None, last=False):
    rows = q.shape[1]
    keys = sum(kv.shape[0] for kv in kvs)
    state = [jax.ShapeDtypeStruct((4, rows, c), F32) for c in (HP, 1, 1)]
    result = [jax.ShapeDtypeStruct((rows // 2, QW), BF)] * 4
    operands = (q, *kvs, *(before or ()))
    return pl.pallas_call(
        functools.partial(attn_kernel, before is not None, last, len(kvs)),
        out_shape=result if last else state,
        in_specs=[vmem()] * len(operands),
        out_specs=[vmem()] * (4 if last else 3),
        scratch_shapes=[pltpu.VMEM((2, rows, keys), F32)],
        compiler_params=params(16),
        cost_estimate=cost(4 * 4 * rows * keys * HP, 5_000_000, 4 * rows * keys),
        name="attention",
    )(*operands)


def pooling(rows):
    r = lax.broadcasted_iota(jnp.int32, (rows // 16, rows), 0)
    c = lax.broadcasted_iota(jnp.int32, (rows // 16, rows), 1)
    return jnp.where(c // 16 == r, 1.0 / 16.0, 0.0).astype(BF)


def head_branch(o, w, head):
    heads = jnp.concatenate([o[:, :HD], o[:, HD:]], axis=0)
    return dot(heads, w[pl.ds(pl.multiple_of(HD * head, 16), HD), :])


def out_rows_kernel(pos, mine, theirs, o0, k0, k1, k3, k2, w, branch, pooled):
    y, g = pos[0], pos[1]
    for k in range(4):
        for back in range(4):
            at = pl.multiple_of(48 * (4 * lax.rem(y + 4 - back, 4) + (g ^ k)), 16)
            for c in range(4):
                top = 192 * (k // 2) + 48 * c
                w[pl.ds(at, 48), QW * c : QW * c + QW] = (mine, theirs)[k % 2][back, top : top + 48, :]
    branch[...] = head_branch(o0, w, y)
    pool = pooling(BLOCK)
    for m, tokens in enumerate((k0, k1, k2, k3)):
        row = (0, 3, 0, 1)[m] * BLOCK
        pooled[m] = dot(pool, tokens[row : row + BLOCK, :])


def out_rows(pos, mine, theirs, o0, toks):
    return pl.pallas_call(
        out_rows_kernel,
        out_shape=[
            jax.ShapeDtypeStruct((HEADS * HD, D), BF),
            jax.ShapeDtypeStruct((BLOCK, D), F32),
            jax.ShapeDtypeStruct((4, BLOCK // 16, QW), F32),
        ],
        in_specs=[smem()] + [vmem()] * 7,
        out_specs=[vmem()] * 3,
        compiler_params=params(8),
        cost_estimate=cost(0, 3_000_000),
        name="out_rows",
    )(pos, mine, theirs, o0, *toks)


def out_kernel(pos, o1, o2, o3, w, first, pooled_tokens, gain, lr, att_out, lr_out):
    y = pos[0]
    branch = first[...]
    for m, o in enumerate((o1, o2, o3)):
        branch = branch + head_branch(o, w, lax.rem(y + m + 1, 4))
    scale = lax.rsqrt(jnp.mean(branch * branch, axis=-1, keepdims=True) + 1e-06)
    att = (branch * scale * gain[...]).astype(BF)
    att_out[...] = att
    pool = pooling(BLOCK)
    sides = None
    for m in range(4):
        at = pl.multiple_of(QW * lax.rem(y + 4 - m, 4), 128)
        pooled = pooled_tokens[m] + dot(pool, att_out[:, pl.ds(at, QW)])
        part = dot(pooled.astype(BF), lr[pl.ds(at, QW), :])
        sides = part if m == 0 else sides + part
    lr_out[...] = sides.astype(BF)


def out_project(pos, os, prepared, gain, lr):
    rows = BLOCK
    return pl.pallas_call(
        out_kernel,
        out_shape=(
            jax.ShapeDtypeStruct((rows, D), BF),
            jax.ShapeDtypeStruct((rows // 16, 256), BF),
        ),
        in_specs=[smem()] + [vmem()] * 8,
        out_specs=(vmem(), vmem()),
        compiler_params=params(12),
        cost_estimate=cost(2 * rows * HEADS * HD * D, 5_000_000, rows),
        name="out_project",
    )(pos, *os, *prepared, gain, lr)


def pair_kernel(rows, cols, r0, r1, r2, r3, w, out, table, mixed):
    for d, r in enumerate((r0, r1, r2, r3)):
        table[8 * d : 8 * d + 8] = r[...].astype(F32).reshape(8, 8, 256)
    tiles = out.shape[0]
    for t in range(tiles):
        left = table[rows[t]][:, :128]
        right = table[cols[t]][:, 128:]
        z = gelu(left[:, None, :] + right[None, :, :])
        mixed[64 * t : 64 * t + 64, :] = z.reshape(64, 128).astype(BF)
    out[...] = dot(mixed[...], w[...]).reshape(tiles, 8, 8, 128).astype(BF)


def pair(rows, cols, sides, w):
    tiles = rows.shape[0]
    return pl.pallas_call(
        pair_kernel,
        out_shape=jax.ShapeDtypeStruct((tiles, 8, 8, 128), BF),
        in_specs=[smem()] * 2 + [vmem()] * 5,
        out_specs=vmem(),
        scratch_shapes=[pltpu.VMEM((32, 8, 256), F32), pltpu.VMEM((tiles * 64, 128), BF)],
        compiler_params=params(8),
        cost_estimate=cost(2 * tiles * 64 * 128 * 128, 1_000_000, tiles * 64 * 128),
        name="pair",
    )(rows, cols, *sides, w)


def shards(
    encoder_in,
    conv_weight,
    norm_gain,
    query_weight,
    key_weight,
    value_weight,
    out_weight,
    post_gain,
    left_weight,
    right_weight,
    pair_weight,
    tile_ids,
):
    seq = lax.axis_index("seq")
    y, j = seq // 4, seq % 4
    pos = jnp.stack([y, j]).astype(jnp.int32)

    msgs = messages(pos, conv_weight, encoder_in, query_weight, key_weight, value_weight)
    out_own = jnp.concatenate([out_weight[:, QW * c : QW * c + QW] for c in range(4)], axis=0)
    out_pair = xor_send(tie(out_own, msgs), 2)
    msgs = [msgs[0]] + [y_send(msgs[d], d) for d in (1, 2, 3)]
    pairs = encoder_in.reshape(BLOCK, 2 * CIN)
    pairs = tie(pairs, msgs[1], msgs[3])
    msgs, out_pair = lax.optimization_barrier((msgs, out_pair))
    w_own, p_own = units(msgs)
    w_across = xor_send(w_own, 2)

    rows_one, rows_three = y_send(pairs, 1), y_send(pairs, 3)
    low, high = halves(rows_one, rows_three, BLOCK // 2)
    rows_low, rows_high = y_send(low, 1), y_send(high, 3)
    w_units = [w_own, xor_send(w_own, 1), w_across, xor_send(w_across, 1)]
    p_own = tie(p_own, w_across)
    p_across = xor_send(p_own, 2)

    first, wall, edges = conv_call(
        conv_first_kernel, "conv_first", (3 * BLOCK, KW * CIN, 288), pos, pairs, rows_one, rows_three, *w_units
    )
    (tok_own,) = conv_call(
        conv_second_kernel, "conv_second", (4 * BLOCK,), pos, rows_low, rows_high, wall, edges, first
    )
    tok_own, p_across = lax.optimization_barrier((tok_own, p_across))
    tok_one, tok_three = y_send(tok_own, 1), y_send(tok_own, 3)
    p_units = [p_own, xor_send(p_own, 1), p_across, xor_send(p_across, 1)]
    tok_low, tok_high = halves(tok_one, tok_three, 2 * BLOCK)
    tok_low, tok_high = y_send(tok_low, 1), y_send(tok_high, 3)
    gain = norm_gain.reshape(4, 1, QW)
    q, kv = qkv(pos, [tok_own, tok_one, tok_three, tok_low, tok_high], gain, p_units)

    kv_across = xor_send(kv, 2)
    out_pair = tie(jnp.concatenate([out_own, out_pair]), kv)
    out_all = [out_pair] + [y_send(out_pair, d) for d in (1, 2, 3)]
    state = attention(q, [kv, xor_send(kv, 1)])
    kv_across, out_all = tie((kv_across, out_all), state)
    kv_diagonal = xor_send(kv_across, 1)
    state = attention(q, [kv_across], state)
    mixed = attention(q, [kv_diagonal], state, True)
    os = [y_send(mixed[d], 4 - d) for d in (1, 2, 3)]
    out_all = jnp.stack(tie(out_all, mixed))
    own_tokens = [tok_own, tok_one, tok_three, tok_high]
    prepared = out_rows(pos, out_all, xor_send(out_all, 1), mixed[0], own_tokens)

    lr = jnp.concatenate([left_weight, right_weight], axis=1)
    attended, sides = out_project(pos, os, prepared, post_gain.reshape(1, D), lr)

    row = jnp.stack([sides] + [xor_send(sides, k) for k in (1, 2, 3)])
    rows_all = [row] + [y_send(row, d) for d in (1, 2, 3)]

    row_table, col_table = np.triu_indices(32)
    matches = tile_ids[:, None] == jnp.arange(row_table.shape[0], dtype=jnp.int32)[None, :]

    def place(number):
        block = jnp.sum(jnp.where(matches, jnp.asarray(number, jnp.int32)[None, :], 0), axis=1)
        owner = block // 2
        back = jnp.mod(y - owner // 4, 4)
        rel = jnp.bitwise_xor(j, owner % 4)
        return (back * 4 + rel) * 2 + block % 2

    pair_tiles = pair(place(row_table), place(col_table), rows_all, pair_weight)
    return (attended, pair_tiles)


def solution(mesh):
    in_specs = (
        P(("dp", "seq"), None),
        P(None, "seq", None),
        P(),
        P("seq", None),
        P("seq", None),
        P("seq", None),
        P("seq", None),
        P(),
        P(),
        P(),
        P(),
        P(("dp", "seq")),
    )
    out_specs = (P(("dp", "seq"), None), P(("dp", "seq"), None, None, None))
    return jax.shard_map(shards, mesh=mesh, in_specs=in_specs, out_specs=out_specs, check_vma=False)
```

```python
import functools

import jax
import jax.numpy as jnp
import numpy as np
from jax import lax
from jax.experimental import pallas as pl
from jax.experimental.pallas import tpu as pltpu
from jax.sharding import PartitionSpec as P

HEADS = 4
BLOCK = 256
HD = 192
HP = 256
D = 1536
QW = 384
CIN = 768
KW = 5
BF = jnp.bfloat16
F32 = jnp.float32
SCALE2 = float(HD ** (-0.5) * np.log2(np.e))


def params(mib):
    return pltpu.CompilerParams(vmem_limit_bytes=mib * 1024 * 1024)


def cost(flops, nbytes, trans=0):
    return pl.CostEstimate(flops=flops, bytes_accessed=nbytes, transcendentals=trans)


def xor_send(x, m):
    return lax.ppermute(x, "seq", [(s, s ^ m) for s in range(16)])


def y_send(x, d):
    return lax.ppermute(x, "seq", [(s, (s + 4 * d) % 16) for s in range(16)])


def tie(x, *others):
    return lax.optimization_barrier((x,) + others)[0]


def gelu(x):
    return 0.5 * x * (1.0 + lax.erf(x * np.float32(np.sqrt(0.5))))


def whole(shape):
    zeros = (0,) * len(shape)
    return pl.BlockSpec(shape, lambda *_: zeros)


def dot(a, b):
    return jnp.dot(a, b, preferred_element_type=F32)


def vmem():
    return pl.BlockSpec(memory_space=pltpu.VMEM)


def smem():
    return pl.BlockSpec(memory_space=pltpu.SMEM)


MSG_EDGE, MSG_KV, MSG_Q, MSG = 240, 256, 352, 400
W_EDGE, W_ALL = 960, 1024
HEAD_ROWS = MSG - MSG_KV


def message_kernel(pos, w, rows, wq, wk, wv, o0, o1, o2, o3, w_in, ends, q_in, k_in, v_in, sems):
    copies = [pltpu.make_async_copy(w.at[t], w_in.at[t], sems.at[t]) for t in range(KW)]
    last = rows.shape[0] - 16
    copies.append(pltpu.make_async_copy(rows.at[pl.ds(0, 16)], ends.at[0], sems.at[KW]))
    copies.append(pltpu.make_async_copy(rows.at[pl.ds(last, 16)], ends.at[1], sems.at[KW + 1]))
    for n, (src, dst) in enumerate(((wq, q_in), (wk, k_in), (wv, v_in))):
        copies.append(pltpu.make_async_copy(src, dst, sems.at[KW + 2 + n]))
    for copy in copies:
        copy.start()
    for copy in copies:
        copy.wait()
    at = lax.broadcasted_iota(jnp.int32, (16, QW), 0)
    edges = jnp.zeros((16, QW), F32)
    first, final = ends[0].astype(F32), ends[1].astype(F32)
    lines = [first[0:1], first[1:2], final[14:15], final[15:16]]
    for n in range(8):
        edges = jnp.where(at == n, lines[n // 2][:, (n % 2) * QW : (n % 2) * QW + QW], edges)
    edges = edges.astype(BF)
    outs = (o0, o1, o2, o3)
    for d, out in enumerate(outs):
        cols = pl.ds(pl.multiple_of(QW * lax.rem(pos[0] + d, 4), 128), QW)
        for t in range(KW):
            out[48 * t : 48 * t + 48, :] = w_in[t, :, cols]
        out[MSG_EDGE:MSG_KV, :] = edges
    for place in range(4):

        @pl.when(pos[0] == place)
        def _():
            for d, out in enumerate(outs):
                head = (place + d) % 4
                cols = slice(HD * head, HD * head + HD)
                out[MSG_KV:MSG_Q, :] = jnp.concatenate([k_in[:, cols], v_in[:, cols]], axis=1)
                out[MSG_Q:MSG, :] = jnp.concatenate([q_in[0:48, cols], q_in[48:96, cols]], axis=1)


def hbm():
    return pl.BlockSpec(memory_space=pltpu.HBM)


def messages(pos, w, rows, wq, wk, wv):
    return pl.pallas_call(
        message_kernel,
        out_shape=[jax.ShapeDtypeStruct((MSG, QW), BF)] * 4,
        in_specs=[smem()] + [hbm()] * 5,
        out_specs=[vmem()] * 4,
        scratch_shapes=[pltpu.VMEM((KW, 48, D), BF), pltpu.VMEM((2, 16, CIN), BF)]
        + [pltpu.VMEM((96, HEADS * HD), BF)] * 3
        + [pltpu.SemaphoreType.DMA((KW + 5,))],
        compiler_params=params(56),
        cost_estimate=cost(0, 3_000_000),
        name="messages",
    )(pos, w, rows, wq, wk, wv)


def unit_kernel(m0, m1, m2, m3, w_out, p_out):
    for d, m in enumerate((m0, m1, m2, m3)):
        w_out[MSG_EDGE * d : MSG_EDGE * d + MSG_EDGE, :] = m[0:MSG_EDGE, :]
        w_out[W_EDGE + 16 * d : W_EDGE + 16 * d + 16, :] = m[MSG_EDGE:MSG_KV, :]
        p_out[HEAD_ROWS * d : HEAD_ROWS * d + HEAD_ROWS, :] = m[MSG_KV:MSG, :]


def units(msgs):
    return pl.pallas_call(
        unit_kernel,
        out_shape=[jax.ShapeDtypeStruct((r, QW), BF) for r in (W_ALL, 4 * HEAD_ROWS)],
        in_specs=[vmem()] * 4,
        out_specs=[vmem()] * 2,
        compiler_params=params(8),
        cost_estimate=cost(0, 1_500_000),
        name="units",
    )(*msgs)


def halves_kernel(one, three, low, high):
    cut = low.shape[0]
    low[...] = one[0:cut, :]
    high[...] = three[cut : 2 * cut, :]


def halves(one, three, cut):
    return pl.pallas_call(
        halves_kernel,
        out_shape=[jax.ShapeDtypeStruct((cut, one.shape[1]), BF)] * 2,
        in_specs=[vmem()] * 2,
        out_specs=[vmem()] * 2,
        compiler_params=params(8),
        cost_estimate=cost(0, 1_000_000),
        name="halves",
    )(one, three)


def place_weights(pos, unit_refs, wall, edges):
    y, g = pos[0], pos[1]
    edges[0:16, :] = jnp.zeros((16, QW), BF)
    edges[272:288, :] = jnp.zeros((16, QW), BF)
    for k, unit in enumerate(unit_refs):
        for back in range(4):
            device = 4 * lax.rem(y + 4 - back, 4) + (g ^ k)
            at = pl.multiple_of(48 * device, 16)
            for t in range(KW):
                start = MSG_EDGE * back + 48 * t
                wall[pl.ds(at + CIN * t, 48), :] = unit[start : start + 48, :]
            lines = W_EDGE + 16 * back
            edges[pl.ds(pl.multiple_of(16 * (device + 1), 16), 16), :] = unit[lines : lines + 16, :]


def block_tokens(device, block, wall, edges):
    at = lax.broadcasted_iota(jnp.int32, (16, 2 * CIN), 0)

    def beside(place, line, row):
        rows = edges[pl.ds(pl.multiple_of(16 * place, 16), 16), :].astype(F32)
        joined = jnp.concatenate([rows[line + n : line + n + 1] for n in range(4)], axis=1)
        return jnp.where(at == row, joined, 0.0).astype(BF)

    near = jnp.concatenate([beside(device, 4, 15), block, beside(device + 2, 0, 0)], axis=0)
    pm, p0, pp = (near[15 + n : 15 + n + BLOCK] for n in range(3))
    halves_of = [v[:, n : n + CIN] for v in (pm, p0, pp) for n in (0, CIN)]
    acc = None
    for t in range(KW):
        pair = jnp.concatenate(halves_of[t : t + 2], axis=0)
        part = dot(pair, wall[CIN * t : CIN * t + CIN, :])
        acc = part if t == 0 else acc + part
    return jnp.maximum(gelu(acc[:BLOCK]), gelu(acc[BLOCK:])).astype(BF)


def device_at(pos, back):
    return 4 * lax.rem(pos[0] + 4 - back, 4) + pos[1]


def conv_first_kernel(pos, b0, b1, b3, u0, u1, u2, u3, out, wall, edges):
    place_weights(pos, (u0, u1, u2, u3), wall, edges)
    for n, (back, block) in enumerate(((0, b0), (1, b1), (3, b3))):
        out[BLOCK * n : BLOCK * n + BLOCK, :] = block_tokens(device_at(pos, back), block[...], wall, edges)


def conv_second_kernel(pos, low, high, wall, edges, first, out):
    block = jnp.concatenate([low[...], high[...]], axis=0)
    out[0 : 2 * BLOCK, :] = first[0 : 2 * BLOCK, :]
    out[2 * BLOCK : 3 * BLOCK, :] = block_tokens(device_at(pos, 2), block, wall, edges)
    out[3 * BLOCK :, :] = first[2 * BLOCK :, :]


def conv_call(kernel, name, shapes, *operands):
    return pl.pallas_call(
        kernel,
        out_shape=[jax.ShapeDtypeStruct((r, QW), BF) for r in shapes],
        in_specs=[smem()] + [vmem()] * (len(operands) - 1),
        out_specs=[vmem()] * len(shapes),
        compiler_params=params(14),
        cost_estimate=cost(2 * 2 * BLOCK * KW * CIN * QW, 8_000_000, 4 * BLOCK * QW),
        name=name,
    )(*operands)


def qkv_kernel(pos, t0, t1, t3, low, high, gain, u0, u1, u2, u3, q_out, kv_out, wall):
    y, g = pos[0], pos[1]
    gap = jnp.zeros((48, HP - HD), BF)
    for k, unit in enumerate((u0, u1, u2, u3)):
        for back in range(4):
            at = pl.multiple_of(96 * (4 * lax.rem(y + 4 - back, 4) + (g ^ k)), 16)
            top = HEAD_ROWS * back
            wall[pl.ds(at, 96), HP:] = unit[top : top + 96, :]
            for side in range(2):
                rows = unit[top + 96 : top + 144, HD * side : HD * side + HD]
                wall[pl.ds(at + 48 * side, 48), 0:HP] = jnp.concatenate([rows, gap], axis=1)

    def tokens(back, block):
        at = (block - back) % 4
        ref = {0: t0, 1: t1, 2: (low, high)[at // 2], 3: t3}[back]
        at = at % 2 if back == 2 else at
        return ref[BLOCK * at : BLOCK * at + BLOCK, :].astype(F32)

    for block in range(4):
        squares = 0.0
        for back in range(4):
            vals = tokens(back, block)
            squares = squares + jnp.sum(vals * vals, axis=-1, keepdims=True)
        scale = lax.rsqrt(squares * np.float32(1.0 / D) + 1e-06)
        acc = 0.0
        for back in range(4):
            place = lax.rem(y + 4 - back, 4)
            normed = (tokens(back, block) * scale * gain[place]).astype(BF)
            acc = acc + dot(normed, wall[pl.ds(pl.multiple_of(QW * place, 128), QW), :])
        done = acc.astype(BF)
        q_out[block] = done[:, :HP]
        kv_out[BLOCK * block : BLOCK * block + BLOCK, :] = done[:, HP:]


def qkv(pos, tokens, gain, head_units):
    rows = tokens[0].shape[0]
    return pl.pallas_call(
        qkv_kernel,
        out_shape=[jax.ShapeDtypeStruct((4, BLOCK, HP), BF), jax.ShapeDtypeStruct((rows, QW), BF)],
        in_specs=[smem()] + [vmem()] * 10,
        out_specs=[vmem()] * 2,
        scratch_shapes=[pltpu.VMEM((D, HP + QW), BF)],
        compiler_params=params(14),
        cost_estimate=cost(2 * rows * D * 640, 6_000_000, rows),
        name="qkv",
    )(pos, *tokens, gain, *head_units)


def attn_kernel(merge, last, n_kv, *refs):
    queries, kvs, rest = refs[0], refs[1 : 1 + n_kv], refs[1 + n_kv :]
    scores = rest[-1]
    for block in range(4):
        q, slot = queries[block], block % 2
        top, at = None, 0
        spans = []
        for kv in kvs:
            n = kv.shape[0]
            s = lax.dot_general(q, kv[:, :HP], (((1,), (1,)), ((), ())), preferred_element_type=F32)
            scores[slot, :, at : at + n] = s
            most = jnp.max(s, axis=-1, keepdims=True)
            top = most if top is None else jnp.maximum(top, most)
            spans.append((kv, at, n))
            at += n
        if merge:
            acc_in, top_in, sum_in = rest[:3]
            top = jnp.maximum(top, top_in[block])
            fade = jnp.exp2((top_in[block] - top) * np.float32(SCALE2))
            total, acc = sum_in[block] * fade, acc_in[block] * fade
        else:
            total, acc = 0.0, 0.0
        for kv, at, n in spans:
            p = jnp.exp2((scores[slot, :, at : at + n] - top) * np.float32(SCALE2))
            total = total + jnp.sum(p, axis=-1, keepdims=True)
            acc = acc + dot(p.astype(BF), kv[:, 128:])
        if last:
            done = (acc / total).astype(BF)[:, HP - HD :]
            half = done.shape[0] // 2
            rest[block - 5][...] = jnp.concatenate([done[:half], done[half:]], axis=1)
        else:
            out, top_out, sum_out = rest[-4:-1]
            out[block] = acc
            top_out[block] = top
            sum_out[block] = total


def attention(q, kvs, before=None, last=False):
    rows = q.shape[1]
    keys = sum(kv.shape[0] for kv in kvs)
    state = [jax.ShapeDtypeStruct((4, rows, c), F32) for c in (HP, 1, 1)]
    result = [jax.ShapeDtypeStruct((rows // 2, QW), BF)] * 4
    operands = (q, *kvs, *(before or ()))
    return pl.pallas_call(
        functools.partial(attn_kernel, before is not None, last, len(kvs)),
        out_shape=result if last else state,
        in_specs=[vmem()] * len(operands),
        out_specs=[vmem()] * (4 if last else 3),
        scratch_shapes=[pltpu.VMEM((2, rows, keys), F32)],
        compiler_params=params(16),
        cost_estimate=cost(4 * 4 * rows * keys * HP, 5_000_000, 4 * rows * keys),
        name="attention",
    )(*operands)


def pooling(rows):
    r = lax.broadcasted_iota(jnp.int32, (rows // 16, rows), 0)
    c = lax.broadcasted_iota(jnp.int32, (rows // 16, rows), 1)
    return jnp.where(c // 16 == r, 1.0 / 16.0, 0.0).astype(BF)


def head_branch(o, w, head):
    heads = jnp.concatenate([o[:, :HD], o[:, HD:]], axis=0)
    return dot(heads, w[pl.ds(pl.multiple_of(HD * head, 16), HD), :])


def out_rows_kernel(pos, mine, theirs, o0, k0, k1, k3, k2, w, branch, pooled):
    y, g = pos[0], pos[1]
    for k in range(4):
        for back in range(4):
            at = pl.multiple_of(48 * (4 * lax.rem(y + 4 - back, 4) + (g ^ k)), 16)
            for c in range(4):
                top = 192 * (k // 2) + 48 * c
                w[pl.ds(at, 48), QW * c : QW * c + QW] = (mine, theirs)[k % 2][back, top : top + 48, :]
    branch[...] = head_branch(o0, w, y)
    pool = pooling(BLOCK)
    for m, tokens in enumerate((k0, k1, k2, k3)):
        row = (0, 3, 0, 1)[m] * BLOCK
        pooled[m] = dot(pool, tokens[row : row + BLOCK, :])


def out_rows(pos, mine, theirs, o0, toks):
    return pl.pallas_call(
        out_rows_kernel,
        out_shape=[
            jax.ShapeDtypeStruct((HEADS * HD, D), BF),
            jax.ShapeDtypeStruct((BLOCK, D), F32),
            jax.ShapeDtypeStruct((4, BLOCK // 16, QW), F32),
        ],
        in_specs=[smem()] + [vmem()] * 7,
        out_specs=[vmem()] * 3,
        compiler_params=params(8),
        cost_estimate=cost(0, 3_000_000),
        name="out_rows",
    )(pos, mine, theirs, o0, *toks)


def out_kernel(pos, o1, o2, o3, w, first, pooled_tokens, gain, lr, att_out, lr_out):
    y = pos[0]
    branch = first[...]
    for m, o in enumerate((o1, o2, o3)):
        branch = branch + head_branch(o, w, lax.rem(y + m + 1, 4))
    scale = lax.rsqrt(jnp.mean(branch * branch, axis=-1, keepdims=True) + 1e-06)
    att = (branch * scale * gain[...]).astype(BF)
    att_out[...] = att
    pool = pooling(BLOCK)
    sides = None
    for m in range(4):
        at = pl.multiple_of(QW * lax.rem(y + 4 - m, 4), 128)
        pooled = pooled_tokens[m] + dot(pool, att_out[:, pl.ds(at, QW)])
        part = dot(pooled.astype(BF), lr[pl.ds(at, QW), :])
        sides = part if m == 0 else sides + part
    lr_out[...] = sides.astype(BF)


def out_project(pos, os, prepared, gain, lr):
    rows = BLOCK
    return pl.pallas_call(
        out_kernel,
        out_shape=(
            jax.ShapeDtypeStruct((rows, D), BF),
            jax.ShapeDtypeStruct((rows // 16, 256), BF),
        ),
        in_specs=[smem()] + [vmem()] * 8,
        out_specs=(vmem(), vmem()),
        compiler_params=params(12),
        cost_estimate=cost(2 * rows * HEADS * HD * D, 5_000_000, rows),
        name="out_project",
    )(pos, *os, *prepared, gain, lr)


def pair_kernel(rows, cols, r0, r1, r2, r3, w, out, table, mixed):
    for d, r in enumerate((r0, r1, r2, r3)):
        table[8 * d : 8 * d + 8] = r[...].astype(F32).reshape(8, 8, 256)
    tiles = out.shape[0]
    for t in range(tiles):
        left = table[rows[t]][:, :128]
        right = table[cols[t]][:, 128:]
        z = gelu(left[:, None, :] + right[None, :, :])
        mixed[64 * t : 64 * t + 64, :] = z.reshape(64, 128).astype(BF)
    out[...] = dot(mixed[...], w[...]).reshape(tiles, 8, 8, 128).astype(BF)


def pair(rows, cols, sides, w):
    tiles = rows.shape[0]
    return pl.pallas_call(
        pair_kernel,
        out_shape=jax.ShapeDtypeStruct((tiles, 8, 8, 128), BF),
        in_specs=[smem()] * 2 + [vmem()] * 5,
        out_specs=vmem(),
        scratch_shapes=[pltpu.VMEM((32, 8, 256), F32), pltpu.VMEM((tiles * 64, 128), BF)],
        compiler_params=params(8),
        cost_estimate=cost(2 * tiles * 64 * 128 * 128, 1_000_000, tiles * 64 * 128),
        name="pair",
    )(rows, cols, *sides, w)


def shards(
    encoder_in,
    conv_weight,
    norm_gain,
    query_weight,
    key_weight,
    value_weight,
    out_weight,
    post_gain,
    left_weight,
    right_weight,
    pair_weight,
    tile_ids,
):
    seq = lax.axis_index("seq")
    y, j = seq // 4, seq % 4
    pos = jnp.stack([y, j]).astype(jnp.int32)

    msgs = messages(pos, conv_weight, encoder_in, query_weight, key_weight, value_weight)
    out_own = jnp.concatenate([out_weight[:, QW * c : QW * c + QW] for c in range(4)], axis=0)
    out_sent, pairs = tie((out_own, encoder_in.reshape(BLOCK, 2 * CIN)), msgs)
    out_pair = xor_send(out_sent, 2)
    msgs = [msgs[0]] + [y_send(msgs[d], d) for d in (1, 2, 3)]
    pairs = tie(pairs, msgs[1], msgs[3])
    msgs, out_pair = lax.optimization_barrier((msgs, out_pair))
    w_own, p_own = units(msgs)
    w_across = xor_send(w_own, 2)

    rows_one, rows_three = y_send(pairs, 1), y_send(pairs, 3)
    low, high = halves(rows_one, rows_three, BLOCK // 2)
    rows_low, rows_high = y_send(low, 1), y_send(high, 3)
    w_units = [w_own, xor_send(w_own, 1), w_across, xor_send(w_across, 1)]
    p_own = tie(p_own, w_across)
    p_across = xor_send(p_own, 2)

    first, wall, edges = conv_call(
        conv_first_kernel, "conv_first", (3 * BLOCK, KW * CIN, 288), pos, pairs, rows_one, rows_three, *w_units
    )
    (tok_own,) = conv_call(
        conv_second_kernel, "conv_second", (4 * BLOCK,), pos, rows_low, rows_high, wall, edges, first
    )
    tok_own, p_across = lax.optimization_barrier((tok_own, p_across))
    tok_one, tok_three = y_send(tok_own, 1), y_send(tok_own, 3)
    p_units = [p_own, xor_send(p_own, 1), p_across, xor_send(p_across, 1)]
    tok_low, tok_high = halves(tok_one, tok_three, 2 * BLOCK)
    tok_low, tok_high = y_send(tok_low, 1), y_send(tok_high, 3)
    gain = norm_gain.reshape(4, 1, QW)
    q, kv = qkv(pos, [tok_own, tok_one, tok_three, tok_low, tok_high], gain, p_units)

    kv_across = xor_send(kv, 2)
    out_pair = tie(jnp.concatenate([out_own, out_pair]), kv)
    out_all = [out_pair] + [y_send(out_pair, d) for d in (1, 2, 3)]
    state = attention(q, [kv, xor_send(kv, 1)])
    kv_across, out_all = tie((kv_across, out_all), state)
    kv_diagonal = xor_send(kv_across, 1)
    state = attention(q, [kv_across], state)
    mixed = attention(q, [kv_diagonal], state, True)
    os = [y_send(mixed[d], 4 - d) for d in (1, 2, 3)]
    out_all = jnp.stack(tie(out_all, mixed))
    own_tokens = [tok_own, tok_one, tok_three, tok_high]
    prepared = out_rows(pos, out_all, xor_send(out_all, 1), mixed[0], own_tokens)

    lr = jnp.concatenate([left_weight, right_weight], axis=1)
    attended, sides = out_project(pos, os, prepared, post_gain.reshape(1, D), lr)

    row = jnp.stack([sides] + [xor_send(sides, k) for k in (1, 2, 3)])
    rows_all = [row] + [y_send(row, d) for d in (1, 2, 3)]

    row_table, col_table = np.triu_indices(32)
    matches = tile_ids[:, None] == jnp.arange(row_table.shape[0], dtype=jnp.int32)[None, :]

    def place(number):
        block = jnp.sum(jnp.where(matches, jnp.asarray(number, jnp.int32)[None, :], 0), axis=1)
        owner = block // 2
        back = jnp.mod(y - owner // 4, 4)
        rel = jnp.bitwise_xor(j, owner % 4)
        return (back * 4 + rel) * 2 + block % 2

    pair_tiles = pair(place(row_table), place(col_table), rows_all, pair_weight)
    return (attended, pair_tiles)


def solution(mesh):
    in_specs = (
        P(("dp", "seq"), None),
        P(None, "seq", None),
        P(),
        P("seq", None),
        P("seq", None),
        P("seq", None),
        P("seq", None),
        P(),
        P(),
        P(),
        P(),
        P(("dp", "seq")),
    )
    out_specs = (P(("dp", "seq"), None), P(("dp", "seq"), None, None, None))
    return jax.shard_map(shards, mesh=mesh, in_specs=in_specs, out_specs=out_specs, check_vma=False)
```
